32 devices in a mesh: role: 2 (over x), seq: 4 (over y, core), head: 4 (over z).
Axes of the slice: x: 2, y: 2, z: 4, core: 2. Of those that a mesh axis runs over, the one named last changes fastest.
Arguments:
- query_heads: bfloat16 [512, 16, 128], P('seq', ('role', 'head')), may hold values from -16 to 16
- key_heads: bfloat16 [512, 8, 128], P('seq', ('role', 'head')), may hold values from -16 to 16
- value_heads: bfloat16 [512, 8, 128], P('seq', ('role', 'head')), may hold values from -6 to 6
- distill_proj: bfloat16 [16, 128, 1024], P(('role', 'head')), may hold values from -6 to 6
- conv_input: bfloat16 [1024, 512], P(('role', 'head'), 'seq'), may hold values from -6 to 6
- gate_input: bfloat16 [1024, 512], P(('role', 'head'), 'seq'), may hold values from -6 to 6
- filter_taps: float32 [1024, 512], P(('role', 'head'), 'seq'), may hold values from -0.25 to 0.25
- skip_gain: float32 [1024], P(('role', 'head')), may hold values from -4 to 4
Outputs:
- grad_input: float32 [1024, 512], P(('role', 'head'), 'seq')
- filter_step: float32 [1024, 512], P(('role', 'head'), 'seq')
The draws below stay inside these ranges and needn't reach their ends.
All inputs are finite; a program needn't handle non-finite values.
Results may differ from the reference program's by a relative error of at most 0.005.
Values may be sent and summed in bfloat16 or wider, within the bound.
A program may use at most 64 MiB of HBM per device.

```python
import math
import jax
import jax.numpy as jnp
from jax import lax

SEQ = 512
QHEADS = 16
KV_HEADS = 8
HEAD_DIM = 128
WINDOW = 4096
CHANNELS = 1024


def draw_query_heads(key, part):
    normal_part = jnp.clip(jax.random.normal(jax.random.fold_in(key, 21), (SEQ, QHEADS, HEAD_DIM), jnp.float32), -6.0, 6.0)
    return normal_part.astype(jnp.bfloat16)


def draw_key_heads(key, part):
    normal_part = jnp.clip(jax.random.normal(jax.random.fold_in(key, 22), (SEQ, KV_HEADS, HEAD_DIM), jnp.float32), -6.0, 6.0)
    return normal_part.astype(jnp.bfloat16)


def raised(entries, own_key, source, target, shards_of, factor):
    owner, partner = [(jnp.arange(entries.shape[axis_at]) // (entries.shape[axis_at] // shards_of)).reshape([-1 if axis == axis_at else 1 for axis in range(entries.ndim)]) for axis_at in (source, target)]
    chosen = jax.random.permutation(own_key, shards_of)[partner]
    strong = (owner == chosen) | (owner == (partner + shards_of // 2) % shards_of)
    return jnp.where(strong, factor * entries, entries)


def block_levels(stream_key, dims, pieces, smallest, top_value):
    factor_of = 1.0
    for dim, shards_of in pieces:
        steps = jax.random.uniform(jax.random.fold_in(jax.random.fold_in(stream_key, 6), dim), (shards_of,), jnp.float32, smallest / len(pieces), top_value / len(pieces))
        factor_of = factor_of * jnp.repeat(jnp.exp(steps), dims[dim] // shards_of).reshape((-1,) + (1,) * (len(dims) - 1 - dim))
    return factor_of


def bell_draw(own_key, shape, scale, reach, split=(), kind=jnp.bfloat16):
    level = block_levels(own_key, shape, split, -0.22, 0.18) if split else 1.0
    drawn = jax.random.normal(own_key, shape, jnp.float32) * scale * level
    return jnp.minimum(jnp.maximum(drawn, -reach), reach).astype(kind)


def noise_with(rng, extent, scale, most, split, heavy, kind=jnp.bfloat16):
    drawn = scale * jax.random.normal(rng, extent, jnp.float32)
    if split:
        drawn = drawn * block_levels(rng, extent, split, -0.22, 0.18)
    return jnp.clip(raised(drawn, jax.random.fold_in(rng, 3), *heavy), -most, most).astype(kind)


def setup_inputs(seed: int = 0) -> dict:
    splits = jax.random.split(jax.random.key(seed), 9)
    return {
        "query_heads": draw_query_heads(jax.random.fold_in(splits[8], 71), 0),
        "key_heads": draw_key_heads(jax.random.fold_in(splits[8], 71), 0),
        "value_heads": bell_draw(splits[2], (SEQ, KV_HEADS, HEAD_DIM), 1.0, 6.0, ((0, 4), (1, 8))),
        "distill_proj": noise_with(splits[3], (QHEADS, HEAD_DIM, CHANNELS), 1.0, 6.0, ((0, 8),), (0, 2, 8, 2.0)),
        "conv_input": bell_draw(splits[4], (CHANNELS, SEQ), 1.0, 6.0, ((0, 8), (1, 4))),
        "gate_input": bell_draw(splits[5], (CHANNELS, SEQ), 1.0, 6.0, ((0, 8), (1, 4))),
        "filter_taps": bell_draw(splits[6], (CHANNELS, SEQ), SEQ ** -0.5, 0.25, ((0, 8), (1, 4)), jnp.float32),
        "skip_gain": bell_draw(splits[7], (CHANNELS,), 1.0, 4.0, ((0, 8),), jnp.float32),
    }


def teacher_target(query_heads, key_heads, value_heads, distill_proj):
    per_group = QHEADS // KV_HEADS
    query_span = math.gcd(SEQ, 512)
    score_scale = HEAD_DIM ** -0.5
    key_pad = jnp.pad(key_heads, ((WINDOW, 0), (0, 0), (0, 0)))
    value_pad = jnp.pad(value_heads, ((WINDOW, 0), (0, 0), (0, 0)))

    def one_block(offset):
        queries = lax.dynamic_slice_in_dim(query_heads, offset, query_span, 0).astype(jnp.float32)
        queries = queries.reshape(query_span, KV_HEADS, per_group, HEAD_DIM)
        key_block = lax.dynamic_slice_in_dim(key_pad, offset, WINDOW + query_span, 0).astype(jnp.float32)
        value_block = lax.dynamic_slice_in_dim(value_pad, offset, WINDOW + query_span, 0).astype(jnp.float32)
        scores = jnp.einsum("qgae,kge->gaqk", queries, key_block) * score_scale
        query_pos = offset + jnp.arange(query_span, dtype=jnp.int32)
        key_pos = offset - WINDOW + jnp.arange(WINDOW + query_span, dtype=jnp.int32)
        in_window = (key_pos[None, :] <= query_pos[:, None]) & (key_pos[None, :] > query_pos[:, None] - WINDOW) & (key_pos[None, :] >= 0)
        row_max = jnp.max(jnp.where(in_window, scores, -jnp.inf), axis=-1, keepdims=True)
        weight = jnp.where(in_window, jnp.exp(scores - row_max), 0.0)
        row_sum = jnp.sum(weight, axis=-1)
        rounded = lax.optimization_barrier(weight.astype(jnp.bfloat16)).astype(jnp.float32)
        weighted = jnp.einsum("gaqk,kge->qgae", rounded, value_block)
        attended = weighted / jnp.transpose(row_sum, (2, 0, 1))[..., None]
        return attended.reshape(query_span, QHEADS, HEAD_DIM).astype(jnp.bfloat16)

    offsets = jnp.arange(SEQ // query_span, dtype=jnp.int32) * query_span
    attended = lax.map(one_block, offsets).reshape(SEQ, QHEADS, HEAD_DIM)
    attended = lax.optimization_barrier(attended).astype(jnp.float32)
    return jnp.einsum("the,hec->ct", attended, distill_proj.astype(jnp.float32))


def student_grads(conv_input, gate_input, filter_taps, skip_gain, target):
    full_len = 2 * SEQ

    def one_group(packed):
        signal, gate_part, taps, skip_part, aimed = packed
        signal = signal.astype(jnp.float32)
        gate_part = gate_part.astype(jnp.float32)
        input_spec = jnp.fft.rfft(signal, n=full_len, axis=-1)
        taps_spec = jnp.fft.rfft(taps, n=full_len, axis=-1)
        convolved = jnp.fft.irfft(input_spec * taps_spec, n=full_len, axis=-1)[:, :SEQ]
        output = gate_part * (convolved + skip_part[:, None] * signal)
        backed = gate_part * (output - aimed)
        back_spec = jnp.fft.rfft(backed, n=full_len, axis=-1)
        corr_input = jnp.fft.irfft(jnp.conj(taps_spec) * back_spec, n=full_len, axis=-1)[:, :SEQ]
        corr_taps = jnp.fft.irfft(jnp.conj(input_spec) * back_spec, n=full_len, axis=-1)[:, :SEQ]
        return skip_part[:, None] * backed + corr_input, corr_taps * (SEQ ** -0.5)

    chan_block = math.gcd(CHANNELS, 64)

    def folded(array):
        return array.reshape((CHANNELS // chan_block, chan_block) + array.shape[1:])

    gradients, updates = lax.map(one_group, (folded(conv_input), folded(gate_input), folded(filter_taps), folded(skip_gain), folded(target)))
    return gradients.reshape(CHANNELS, SEQ), updates.reshape(CHANNELS, SEQ)


def reference(query_heads, key_heads, value_heads, distill_proj, conv_input, gate_input, filter_taps, skip_gain):
    target = teacher_target(query_heads, key_heads, value_heads, distill_proj)
    grad_input, filter_step = student_grads(conv_input, gate_input, filter_taps, skip_gain, target)
    return (grad_input, filter_step)
```

```python
import functools
import math

import jax
import jax.numpy as jnp
import ml_dtypes
import numpy as np
from jax import lax
from jax.experimental import pallas as pl
from jax.experimental.pallas import tpu as pltpu
from jax.sharding import PartitionSpec as P

WINDOW = 4096
MESH = pl.DeviceIdType.MESH
highest = lax.Precision.HIGHEST


def shifted(value, axis, steps):
    count = lax.axis_size(axis)
    leading, last = (max(0, -steps), min(count, count - steps))
    return lax.ppermute(value, axis, [(source, source + steps) for source in range(leading, last)])


def angle_table(row_ids, col_ids, length):
    product = row_ids[:, None] * col_ids[None, :] % length
    quarter = length // 4
    eighth = length // 8
    quadrant = product // quarter
    within = product % quarter
    flipped = within > eighth
    reduced = jnp.where(flipped, quarter - within, within)
    angles = reduced.astype(jnp.float32) * (2.0 * math.pi / length)
    base_cos = jnp.cos(angles)
    base_sin = jnp.sin(angles)
    first_cos = jnp.where(flipped, base_sin, base_cos)
    first_sin = jnp.where(flipped, base_cos, base_sin)
    cosine = jnp.where(
        quadrant == 0,
        first_cos,
        jnp.where(quadrant == 1, -first_sin, jnp.where(quadrant == 2, -first_cos, first_sin)),
    )
    sine_part = jnp.where(
        quadrant == 0,
        first_sin,
        jnp.where(quadrant == 1, first_cos, jnp.where(quadrant == 2, -first_sin, -first_cos)),
    )
    return (cosine, sine_part)


def spread_rows(stacked):
    pieces = stacked.shape[2]
    cosine, sine_part = angle_table(
        jnp.arange(2 * pieces, dtype=jnp.int32), jnp.arange(pieces, dtype=jnp.int32), 2 * pieces
    )
    real_part = jnp.einsum("kd,ncdr->nckr", cosine, stacked, precision=highest)
    imag_part = -jnp.einsum("kd,ncdr->nckr", sine_part, stacked, precision=highest)
    return (real_part, imag_part)


def twist(real_part, imag_part, freq_ids, time_ids, length, turning):
    cosine, sine_part = angle_table(freq_ids, time_ids, length)
    return (
        real_part * cosine - turning * imag_part * sine_part,
        imag_part * cosine + turning * real_part * sine_part,
    )


def along_block(real_part, imag_part, turning):
    length = real_part.shape[-1]
    cosine, sine_part = angle_table(
        jnp.arange(length, dtype=jnp.int32), jnp.arange(length, dtype=jnp.int32), length
    )
    out_real = jnp.einsum(
        "nckb,bj->nckj", real_part, cosine, precision=highest
    ) - turning * jnp.einsum("nckb,bj->nckj", imag_part, sine_part, precision=highest)
    out_imag = jnp.einsum(
        "nckb,bj->nckj", imag_part, cosine, precision=highest
    ) + turning * jnp.einsum("nckb,bj->nckj", real_part, sine_part, precision=highest)
    return (out_real, out_imag)


def gather_rows(real_part, imag_part, length):
    doubled = real_part.shape[2]
    cosine, sine_part = angle_table(
        jnp.arange(doubled // 2, dtype=jnp.int32), jnp.arange(doubled, dtype=jnp.int32), doubled
    )
    signal = jnp.einsum("dk,nckr->ncdr", cosine, real_part, precision=highest) - jnp.einsum(
        "dk,nckr->ncdr", sine_part, imag_part, precision=highest
    )
    return signal / length


def student(signal, gate_part, taps, target, skip_part, forward, inverse, seq_total):
    spec_real, spec_imag = forward(jnp.stack([signal, taps]))
    input_re, taps_re = (spec_real[0], spec_real[1])
    input_im, taps_im = (spec_imag[0], spec_imag[1])
    conv_re = input_re * taps_re - input_im * taps_im
    conv_im = input_re * taps_im + input_im * taps_re
    convolved = inverse(conv_re[None], conv_im[None])[0]
    output = gate_part * (convolved + skip_part[:, None] * signal)
    backed = gate_part * (output - target)
    back_real, back_imag = forward(backed[None])
    back_re, back_im = (back_real[0], back_imag[0])
    left_re = taps_re * back_re + taps_im * back_im
    left_im = taps_re * back_im - taps_im * back_re
    right_re = input_re * back_re + input_im * back_im
    right_im = input_re * back_im - input_im * back_re
    corrected = inverse(jnp.stack([left_re, right_re]), jnp.stack([left_im, right_im]))
    grad_input = skip_part[:, None] * backed + corrected[0]
    filter_step = corrected[1] * seq_total ** (-0.5)
    return (grad_input, filter_step)


def body(
    query_heads,
    key_heads,
    value_heads,
    distill_proj,
    conv_input,
    gate_input,
    filter_taps,
    skip_gain,
):
    shard_len = query_heads.shape[0]
    kv_local = key_heads.shape[1]
    per_group = query_heads.shape[1] // kv_local
    head_dim = query_heads.shape[2]
    devices = lax.axis_size("seq")
    seq_rank = lax.axis_index("seq")
    shards = min((WINDOW + shard_len - 1) // shard_len, devices - 1)
    per_step = max(1, 512 // shard_len)
    total_shards = -(-(shards + 1) // per_step) * per_step
    own_block = jnp.stack([key_heads, value_heads])
    buffer = jnp.concatenate(
        [jnp.zeros((total_shards - 1,) + own_block.shape, jnp.bfloat16), own_block[None]], axis=0
    )

    def fetch(step_id, carried):
        current, stored = carried
        current = shifted(current, "seq", 1)
        stored = lax.dynamic_update_index_in_dim(stored, current, total_shards - 1 - step_id, 0)
        return (current, stored)

    buffer = lax.fori_loop(1, shards + 1, fetch, (own_block, buffer))[1]
    key_span = per_step * shard_len
    blocks = total_shards // per_step
    keys_all = buffer[:, 0].reshape(blocks, key_span, kv_local, head_dim)
    values_all = buffer[:, 1].reshape(blocks, key_span, kv_local, head_dim)
    first_key = (seq_rank + 1 - total_shards) * shard_len
    query_pos = seq_rank * shard_len + jnp.arange(shard_len, dtype=jnp.int32)
    queries = query_heads.reshape(shard_len, kv_local, per_group, head_dim)
    score_scale = head_dim ** (-0.5)
    block_ids = jnp.arange(blocks, dtype=jnp.int32)

    def online_step(carried, element):
        row_max, row_sum, weighted = carried
        block_id, key_block, value_block = element
        scores = (
            jnp.einsum("qgae,kge->gaqk", queries, key_block, preferred_element_type=jnp.float32)
            * score_scale
        )
        key_pos = first_key + block_id * key_span + jnp.arange(key_span, dtype=jnp.int32)
        in_window = (
            (key_pos[None, :] <= query_pos[:, None])
            & (key_pos[None, :] > query_pos[:, None] - WINDOW)
            & (key_pos[None, :] >= 0)
        )
        new_max = jnp.maximum(row_max, jnp.max(jnp.where(in_window, scores, -jnp.inf), axis=-1))
        safe_max = jnp.where(new_max == -jnp.inf, 0.0, new_max)
        rescale = jnp.exp(row_max - safe_max)
        weight = jnp.where(in_window, jnp.exp(scores - safe_max[..., None]), 0.0)
        row_sum = row_sum * rescale + jnp.sum(weight, axis=-1)
        weighted = weighted * jnp.transpose(rescale, (2, 0, 1))[..., None] + jnp.einsum(
            "gaqk,kge->qgae",
            weight.astype(jnp.bfloat16),
            value_block,
            preferred_element_type=jnp.float32,
        )
        return ((new_max, row_sum, weighted), None)

    start_state = (
        jnp.full((kv_local, per_group, shard_len), -jnp.inf, jnp.float32),
        jnp.zeros((kv_local, per_group, shard_len), jnp.float32),
        jnp.zeros((shard_len, kv_local, per_group, head_dim), jnp.float32),
    )
    final_state = lax.scan(online_step, start_state, (block_ids, keys_all, values_all))[0]
    row_sum, weighted = (final_state[1], final_state[2])
    attended = (
        (weighted / jnp.transpose(row_sum, (2, 0, 1))[..., None])
        .reshape(shard_len, kv_local * per_group, head_dim)
        .astype(jnp.bfloat16)
    )
    target = lax.psum_scatter(
        jnp.einsum("the,hec->ct", attended, distill_proj, preferred_element_type=jnp.float32),
        ("role", "head"),
        scatter_dimension=0,
        tiled=True,
    )
    signal = conv_input.astype(jnp.float32)
    gate_part = gate_input.astype(jnp.float32)
    full_len = 2 * devices * shard_len
    seq_total = devices * shard_len
    freq_all = jnp.arange(2 * devices, dtype=jnp.int32)
    time_all = jnp.arange(shard_len, dtype=jnp.int32)
    part_len = shard_len // devices
    freq_mine = 2 * seq_rank + jnp.arange(2, dtype=jnp.int32)
    time_mine = seq_rank * part_len + jnp.arange(part_len, dtype=jnp.int32)

    def to_rows(stacked):
        return lax.all_to_all(stacked, "seq", split_axis=3, concat_axis=2, tiled=True)

    def to_cols(stacked):
        return lax.all_to_all(stacked, "seq", split_axis=2, concat_axis=3, tiled=True)

    def forward(stacked):
        pieces = stacked.shape[0]
        arrived = to_rows(stacked[:, :, None, :])
        real_part, imag_part = spread_rows(arrived)
        real_part, imag_part = twist(real_part, imag_part, freq_all, time_mine, full_len, -1.0)
        joined = to_cols(jnp.concatenate([real_part, imag_part], axis=0))
        return along_block(joined[:pieces], joined[pieces:], -1.0)

    def inverse(real_part, imag_part):
        pieces = real_part.shape[0]
        real_part, imag_part = along_block(real_part, imag_part, 1.0)
        real_part, imag_part = twist(real_part, imag_part, freq_mine, time_all, full_len, 1.0)
        arrived = to_rows(jnp.concatenate([real_part, imag_part], axis=0))
        rebuilt = gather_rows(arrived[:pieces], arrived[pieces:], full_len)
        return to_cols(rebuilt)[:, :, 0, :]

    grad_input, filter_step = student(
        signal, gate_part, filter_taps, target, skip_gain, forward, inverse, seq_total
    )
    return (grad_input, filter_step)


def half_step_table(length):
    product = np.arange(length)[:, None] * (2 * np.arange(length)[None, :] + 1) % (4 * length)
    angle = product * (math.pi / (2 * length))
    whole = np.concatenate([np.cos(angle), np.sin(angle)], axis=1)
    upper = whole.astype(ml_dtypes.bfloat16)
    lower = (whole - upper.astype(np.float64)).astype(ml_dtypes.bfloat16)
    return np.stack([upper, lower])


def fits_fused(query_heads, key_heads, value_heads, distill_proj, conv_input, gate_input, filter_taps, skip_gain):
    seq_total = lax.axis_size("seq") * query_heads.shape[0]
    groups = lax.axis_size("role") * lax.axis_size("head")
    chan_local = conv_input.shape[0]
    return (
        seq_total <= min(WINDOW, 1024)
        and query_heads.shape[0] % 128 == 0
        and key_heads.shape[1] == 1
        and key_heads.shape[2] % 128 == 0
        and chan_local % 128 == 0
        and chan_local * groups == distill_proj.shape[2]
    )


def dot_nt(left, right):
    return lax.dot_general(left, right, (((1,), (1,)), ((), ())), preferred_element_type=jnp.float32)


def forward(rows, table_buf, where):
    upper = jnp.dot(rows, table_buf[0, where, :], preferred_element_type=jnp.float32)
    return upper + jnp.dot(rows, table_buf[1, where, :], preferred_element_type=jnp.float32)


def inverse(spec, turned_buf):
    upper = spec.astype(jnp.bfloat16)
    lower = (spec - upper.astype(jnp.float32)).astype(jnp.bfloat16)
    both = jnp.concatenate([upper, lower], axis=0)
    first = jnp.dot(both, turned_buf[0], preferred_element_type=jnp.float32)
    second = jnp.dot(upper, turned_buf[1], preferred_element_type=jnp.float32)
    return first[: spec.shape[0]] + (first[spec.shape[0]:] + second)


def fused_kernel(
    seq_n, role_n, head_n, heads,
    query_hbm, key_hbm, value_hbm, proj_hbm, signal_hbm, gate_hbm, taps_hbm, skip_hbm, table_hbm, turned_hbm,
    grad_ref, step_ref,
    query_buf, key_buf, value_buf, proj_buf, gate_buf, taps_buf, skip_buf, table_buf, turned_buf,
    pair_buf, spec_buf, out_buf, part_send, part_recv, back_buf,
    local_sem, gather_send, gather_recv, part_send_sem, part_recv_sem, back_send, back_recv,
):
    group_n = role_n * head_n
    mine = lax.axis_index("seq")
    group = lax.axis_index("role") * head_n + lax.axis_index("head")
    span = key_hbm.shape[0]
    chans = gate_buf.shape[0]
    seq_total = seq_n * span
    head_dim = key_hbm.shape[1]
    here = pl.ds(pl.multiple_of(mine * span, span), span)

    def place(rank):
        return pl.ds(pl.multiple_of(rank * span, span), span)

    def seq_peer(step):
        return lax.rem(mine + step, seq_n)

    def seq_from(step):
        return lax.rem(mine + seq_n - step, seq_n)

    def group_peer(step):
        other = lax.rem(group + step, group_n)
        return other, {"role": other // head_n, "head": lax.rem(other, head_n)}

    def group_from(step):
        return lax.rem(group + group_n - step, group_n)

    signal_rows, taps_rows = pl.ds(0, chans), pl.ds(chans, chans)
    locals_ = [
        pltpu.make_async_copy(source, target, local_sem.at[index])
        for index, (source, target) in enumerate([
            (taps_hbm, taps_buf),
            (query_hbm, query_buf),
            (key_hbm, key_buf.at[here]),
            (value_hbm, value_buf.at[here]),
            (signal_hbm, pair_buf.at[signal_rows, here]),
            (proj_hbm, proj_buf),
            (gate_hbm, gate_buf),
            (skip_hbm, skip_buf),
            (table_hbm, table_buf),
            (turned_hbm.at[:, :, here], turned_buf),
        ])
    ]
    for copy in locals_:
        copy.start()
    taps_copy, query_copy, key_copy, value_copy, signal_copy, proj_copy, gate_copy, skip_copy, table_copy, turned_copy = locals_

    barrier = pltpu.get_barrier_semaphore()
    for step in range(1, seq_n):
        pl.semaphore_signal(barrier, inc=1, device_id={"seq": seq_peer(step)}, device_id_type=MESH)
    for step in range(1, group_n):
        pl.semaphore_signal(barrier, inc=1, device_id=group_peer(step)[1], device_id_type=MESH)
    taps_copy.wait()
    pair_buf[taps_rows, here] = taps_buf[...].astype(jnp.bfloat16)
    rows = query_buf.shape[0]
    row_id = lax.broadcasted_iota(jnp.int32, (rows, rows), 0)
    col_id = lax.broadcasted_iota(jnp.int32, (rows, rows), 1)
    wanted = (row_id % span) * heads + row_id // span
    order = jnp.where(col_id == wanted, 1.0, 0.0).astype(jnp.bfloat16)
    query_copy.wait()
    queries = jnp.dot(order, query_buf[...], preferred_element_type=jnp.float32).astype(jnp.bfloat16)
    pl.semaphore_wait(barrier, seq_n + group_n - 2)

    def gather(kind, step, source, target):
        return pltpu.make_async_remote_copy(
            src_ref=source,
            dst_ref=target,
            send_sem=gather_send.at[kind, step],
            recv_sem=gather_recv.at[kind, step],
            device_id={"seq": seq_peer(step)},
            device_id_type=MESH,
        )

    far_first = sorted(range(1, seq_n), key=lambda step: abs(2 * step - seq_n))
    sends = []
    for kind, source, target in (
        (0, key_hbm, key_buf.at[here]),
        (1, value_hbm, value_buf.at[here]),
        (2, signal_hbm, pair_buf.at[signal_rows, here]),
        (3, pair_buf.at[taps_rows, here], pair_buf.at[taps_rows, here]),
    ):
        for step in far_first:
            copy = gather(kind, step, source, target)
            copy.start()
            sends.append(copy)

    key_copy.wait()
    value_copy.wait()
    for step in range(1, seq_n):
        gather(0, step, key_hbm, key_buf.at[place(seq_from(step))]).wait_recv()
    scores = dot_nt(queries, key_buf[...]) * (head_dim ** -0.5)
    query_pos = mine * span + lax.broadcasted_iota(jnp.int32, scores.shape, 0) % span
    key_pos = lax.broadcasted_iota(jnp.int32, scores.shape, 1)
    live = key_pos <= query_pos
    row_max = jnp.max(jnp.where(live, scores, -jnp.inf), axis=1, keepdims=True)
    weight = jnp.where(live, jnp.exp(scores - row_max), 0.0)
    row_sum = jnp.sum(weight, axis=1, keepdims=True)
    for step in range(1, seq_n):
        gather(1, step, value_hbm, value_buf.at[place(seq_from(step))]).wait_recv()
    weighted = jnp.dot(weight.astype(jnp.bfloat16), value_buf[...], preferred_element_type=jnp.float32)
    attended = (weighted / row_sum).astype(jnp.bfloat16)

    proj_copy.wait()
    partial = jnp.dot(attended[:span], proj_buf[0], preferred_element_type=jnp.float32)
    for head in range(1, heads):
        partial = partial + jnp.dot(
            attended[head * span:(head + 1) * span], proj_buf[head], preferred_element_type=jnp.float32
        )
    for block in range(group_n):
        part_send[block] = partial[:, block * chans:(block + 1) * chans].astype(jnp.bfloat16)

    def part_copy(step, slot):
        other, device = group_peer(step)
        return pltpu.make_async_remote_copy(
            src_ref=part_send.at[other],
            dst_ref=part_recv.at[slot],
            send_sem=part_send_sem.at[step],
            recv_sem=part_recv_sem.at[step],
            device_id=device,
            device_id_type=MESH,
        )

    for step in range(1, group_n):
        copy = part_copy(step, step)
        copy.start()
        sends.append(copy)

    signal_copy.wait()
    for step in range(1, seq_n):
        gather(2, step, signal_hbm, pair_buf.at[signal_rows, place(seq_from(step))]).wait_recv()
        gather(3, step, pair_buf.at[taps_rows, here], pair_buf.at[taps_rows, place(seq_from(step))]).wait_recv()
    table_copy.wait()
    turned_copy.wait()
    gate_copy.wait()
    skip_copy.wait()
    spec_buf[...] = forward(pair_buf[...], table_buf, slice(None))
    low, high = pl.ds(0, seq_total), pl.ds(seq_total, seq_total)
    input_c, input_s = spec_buf[signal_rows, low], spec_buf[signal_rows, high]
    taps_c, taps_s = spec_buf[taps_rows, low], spec_buf[taps_rows, high]
    conv_spec = jnp.concatenate(
        [input_c * taps_c - input_s * taps_s, input_c * taps_s + input_s * taps_c], axis=1
    )
    conv = inverse(conv_spec, turned_buf) * (1.0 / seq_total)
    skip = jnp.transpose(jnp.broadcast_to(skip_buf[...], (span, chans)))
    gate = gate_buf[...].astype(jnp.float32)
    out_buf[...] = gate * (conv + skip * pair_buf[signal_rows, here].astype(jnp.float32))

    target = part_send[group].astype(jnp.float32)
    for step in range(1, group_n):
        part_copy(step, step).wait_recv()
        target = target + part_recv[step].astype(jnp.float32)
    back = gate * (out_buf[...] - jnp.transpose(target))
    back_buf[:, here] = back.astype(jnp.bfloat16)

    def back_copy(step, owner):
        where = place(owner)
        return pltpu.make_async_remote_copy(
            src_ref=back_buf.at[:, here],
            dst_ref=back_buf.at[:, where],
            send_sem=back_send.at[step],
            recv_sem=back_recv.at[owner],
            device_id={"seq": seq_peer(step)},
            device_id_type=MESH,
        )

    for step in far_first:
        copy = back_copy(step, mine)
        copy.start()
        sends.append(copy)
    width = 2 if seq_n % 2 == 0 else 1
    back_spec = 0.0
    for step in range(seq_n // width):
        first = lax.rem(mine // width + step, seq_n // width) * width
        for owner in ([lax.rem(mine + 1, 2) + first] if step == 0 and width == 2 else []) + (
            [first + inner for inner in range(width)] if step else []
        ):
            back_copy(1, owner).wait_recv()
        where = pl.ds(pl.multiple_of(first * span, width * span), width * span)
        back_spec = back_spec + forward(back_buf[:, where], table_buf, where)
    back_c, back_s = back_spec[:, :seq_total], back_spec[:, seq_total:]

    def correlation(rows):
        first_c, first_s = spec_buf[rows, low], spec_buf[rows, high]
        return jnp.concatenate([first_c * back_c + first_s * back_s, first_c * back_s - first_s * back_c], axis=1)

    lags = inverse(jnp.concatenate([correlation(taps_rows), correlation(signal_rows)], axis=0), turned_buf)
    grad_ref[...] = skip * back + lags[:chans] * (1.0 / seq_total)
    step_ref[...] = lags[chans:] * (seq_total ** -1.5)
    for copy in sends:
        copy.wait_send()


def fused_body(query_heads, key_heads, value_heads, distill_proj, conv_input, gate_input, filter_taps, skip_gain):
    span, heads, head_dim = query_heads.shape
    seq_n, role_n, head_n = (lax.axis_size(axis) for axis in ("seq", "role", "head"))
    group_n = role_n * head_n
    seq_total = seq_n * span
    chans = conv_input.shape[0]
    table_terms = half_step_table(seq_total)
    table = jnp.asarray(table_terms)
    turned = jnp.asarray(np.ascontiguousarray(np.swapaxes(table_terms, 1, 2)))
    in_hbm = pl.BlockSpec(memory_space=pltpu.HBM)
    vmem = pl.BlockSpec(memory_space=pltpu.VMEM)
    bf16, f32 = jnp.bfloat16, jnp.float32
    dma = pltpu.SemaphoreType.DMA
    return pl.pallas_call(
        functools.partial(fused_kernel, seq_n, role_n, head_n, heads),
        out_shape=[jax.ShapeDtypeStruct((chans, span), f32)] * 2,
        in_specs=[in_hbm] * 10,
        out_specs=[vmem, vmem],
        scratch_shapes=[
            pltpu.VMEM((span * heads, head_dim), bf16),
            pltpu.VMEM((seq_total, head_dim), bf16),
            pltpu.VMEM((seq_total, head_dim), bf16),
            pltpu.VMEM(distill_proj.shape, bf16),
            pltpu.VMEM((chans, span), bf16),
            pltpu.VMEM((chans, span), f32),
            pltpu.VMEM((1, chans), f32),
            pltpu.VMEM(table.shape, bf16),
            pltpu.VMEM((2, 2 * seq_total, span), bf16),
            pltpu.VMEM((2 * chans, seq_total), bf16),
            pltpu.VMEM((2 * chans, 2 * seq_total), f32),
            pltpu.VMEM((chans, span), f32),
            pltpu.VMEM((group_n, span, chans), bf16),
            pltpu.VMEM((group_n, span, chans), bf16),
            pltpu.VMEM((chans, seq_total), bf16),
            dma((10,)),
            dma((4, seq_n)),
            dma((4, seq_n)),
            dma((group_n,)),
            dma((group_n,)),
            dma((seq_n,)),
            dma((seq_n,)),
        ],
        compiler_params=pltpu.CompilerParams(
            collective_id=0, has_side_effects=True, vmem_limit_bytes=63 * 1024 * 1024
        ),
    )(
        query_heads.reshape(span * heads, head_dim),
        key_heads.reshape(span, head_dim),
        value_heads.reshape(span, head_dim),
        distill_proj,
        conv_input,
        gate_input,
        filter_taps,
        skip_gain.reshape(1, chans),
        table,
        turned,
    )


def solution(mesh):
    in_specs = (
        P("seq", ("role", "head"), None),
        P("seq", ("role", "head"), None),
        P("seq", ("role", "head"), None),
        P(("role", "head"), None, None),
        P(("role", "head"), "seq"),
        P(("role", "head"), "seq"),
        P(("role", "head"), "seq"),
        P(("role", "head")),
    )
    out_specs = (P(("role", "head"), "seq"), P(("role", "head"), "seq"))
    def chosen(*arrays):
        return fused_body(*arrays) if fits_fused(*arrays) else body(*arrays)

    return jax.shard_map(chosen, mesh=mesh, in_specs=in_specs, out_specs=out_specs, check_vma=False)
```

```python
import functools
import math

import jax
import jax.numpy as jnp
import ml_dtypes
import numpy as np
from jax import lax
from jax.experimental import pallas as pl
from jax.experimental.pallas import tpu as pltpu
from jax.sharding import PartitionSpec as P

WINDOW = 4096
MESH = pl.DeviceIdType.MESH
highest = lax.Precision.HIGHEST


def shifted(value, axis, steps):
    count = lax.axis_size(axis)
    leading, last = (max(0, -steps), min(count, count - steps))
    return lax.ppermute(value, axis, [(source, source + steps) for source in range(leading, last)])


def angle_table(row_ids, col_ids, length):
    product = row_ids[:, None] * col_ids[None, :] % length
    quarter = length // 4
    eighth = length // 8
    quadrant = product // quarter
    within = product % quarter
    flipped = within > eighth
    reduced = jnp.where(flipped, quarter - within, within)
    angles = reduced.astype(jnp.float32) * (2.0 * math.pi / length)
    base_cos = jnp.cos(angles)
    base_sin = jnp.sin(angles)
    first_cos = jnp.where(flipped, base_sin, base_cos)
    first_sin = jnp.where(flipped, base_cos, base_sin)
    cosine = jnp.where(
        quadrant == 0,
        first_cos,
        jnp.where(quadrant == 1, -first_sin, jnp.where(quadrant == 2, -first_cos, first_sin)),
    )
    sine_part = jnp.where(
        quadrant == 0,
        first_sin,
        jnp.where(quadrant == 1, first_cos, jnp.where(quadrant == 2, -first_sin, -first_cos)),
    )
    return (cosine, sine_part)


def spread_rows(stacked):
    pieces = stacked.shape[2]
    cosine, sine_part = angle_table(
        jnp.arange(2 * pieces, dtype=jnp.int32), jnp.arange(pieces, dtype=jnp.int32), 2 * pieces
    )
    real_part = jnp.einsum("kd,ncdr->nckr", cosine, stacked, precision=highest)
    imag_part = -jnp.einsum("kd,ncdr->nckr", sine_part, stacked, precision=highest)
    return (real_part, imag_part)


def twist(real_part, imag_part, freq_ids, time_ids, length, turning):
    cosine, sine_part = angle_table(freq_ids, time_ids, length)
    return (
        real_part * cosine - turning * imag_part * sine_part,
        imag_part * cosine + turning * real_part * sine_part,
    )


def along_block(real_part, imag_part, turning):
    length = real_part.shape[-1]
    cosine, sine_part = angle_table(
        jnp.arange(length, dtype=jnp.int32), jnp.arange(length, dtype=jnp.int32), length
    )
    out_real = jnp.einsum(
        "nckb,bj->nckj", real_part, cosine, precision=highest
    ) - turning * jnp.einsum("nckb,bj->nckj", imag_part, sine_part, precision=highest)
    out_imag = jnp.einsum(
        "nckb,bj->nckj", imag_part, cosine, precision=highest
    ) + turning * jnp.einsum("nckb,bj->nckj", real_part, sine_part, precision=highest)
    return (out_real, out_imag)


def gather_rows(real_part, imag_part, length):
    doubled = real_part.shape[2]
    cosine, sine_part = angle_table(
        jnp.arange(doubled // 2, dtype=jnp.int32), jnp.arange(doubled, dtype=jnp.int32), doubled
    )
    signal = jnp.einsum("dk,nckr->ncdr", cosine, real_part, precision=highest) - jnp.einsum(
        "dk,nckr->ncdr", sine_part, imag_part, precision=highest
    )
    return signal / length


def student(signal, gate_part, taps, target, skip_part, forward, inverse, seq_total):
    spec_real, spec_imag = forward(jnp.stack([signal, taps]))
    input_re, taps_re = (spec_real[0], spec_real[1])
    input_im, taps_im = (spec_imag[0], spec_imag[1])
    conv_re = input_re * taps_re - input_im * taps_im
    conv_im = input_re * taps_im + input_im * taps_re
    convolved = inverse(conv_re[None], conv_im[None])[0]
    output = gate_part * (convolved + skip_part[:, None] * signal)
    backed = gate_part * (output - target)
    back_real, back_imag = forward(backed[None])
    back_re, back_im = (back_real[0], back_imag[0])
    left_re = taps_re * back_re + taps_im * back_im
    left_im = taps_re * back_im - taps_im * back_re
    right_re = input_re * back_re + input_im * back_im
    right_im = input_re * back_im - input_im * back_re
    corrected = inverse(jnp.stack([left_re, right_re]), jnp.stack([left_im, right_im]))
    grad_input = skip_part[:, None] * backed + corrected[0]
    filter_step = corrected[1] * seq_total ** (-0.5)
    return (grad_input, filter_step)


def body(
    query_heads,
    key_heads,
    value_heads,
    distill_proj,
    conv_input,
    gate_input,
    filter_taps,
    skip_gain,
):
    shard_len = query_heads.shape[0]
    kv_local = key_heads.shape[1]
    per_group = query_heads.shape[1] // kv_local
    head_dim = query_heads.shape[2]
    devices = lax.axis_size("seq")
    seq_rank = lax.axis_index("seq")
    shards = min((WINDOW + shard_len - 1) // shard_len, devices - 1)
    per_step = max(1, 512 // shard_len)
    total_shards = -(-(shards + 1) // per_step) * per_step
    own_block = jnp.stack([key_heads, value_heads])
    buffer = jnp.concatenate(
        [jnp.zeros((total_shards - 1,) + own_block.shape, jnp.bfloat16), own_block[None]], axis=0
    )

    def fetch(step_id, carried):
        current, stored = carried
        current = shifted(current, "seq", 1)
        stored = lax.dynamic_update_index_in_dim(stored, current, total_shards - 1 - step_id, 0)
        return (current, stored)

    buffer = lax.fori_loop(1, shards + 1, fetch, (own_block, buffer))[1]
    key_span = per_step * shard_len
    blocks = total_shards // per_step
    keys_all = buffer[:, 0].reshape(blocks, key_span, kv_local, head_dim)
    values_all = buffer[:, 1].reshape(blocks, key_span, kv_local, head_dim)
    first_key = (seq_rank + 1 - total_shards) * shard_len
    query_pos = seq_rank * shard_len + jnp.arange(shard_len, dtype=jnp.int32)
    queries = query_heads.reshape(shard_len, kv_local, per_group, head_dim)
    score_scale = head_dim ** (-0.5)
    block_ids = jnp.arange(blocks, dtype=jnp.int32)

    def online_step(carried, element):
        row_max, row_sum, weighted = carried
        block_id, key_block, value_block = element
        scores = (
            jnp.einsum("qgae,kge->gaqk", queries, key_block, preferred_element_type=jnp.float32)
            * score_scale
        )
        key_pos = first_key + block_id * key_span + jnp.arange(key_span, dtype=jnp.int32)
        in_window = (
            (key_pos[None, :] <= query_pos[:, None])
            & (key_pos[None, :] > query_pos[:, None] - WINDOW)
            & (key_pos[None, :] >= 0)
        )
        new_max = jnp.maximum(row_max, jnp.max(jnp.where(in_window, scores, -jnp.inf), axis=-1))
        safe_max = jnp.where(new_max == -jnp.inf, 0.0, new_max)
        rescale = jnp.exp(row_max - safe_max)
        weight = jnp.where(in_window, jnp.exp(scores - safe_max[..., None]), 0.0)
        row_sum = row_sum * rescale + jnp.sum(weight, axis=-1)
        weighted = weighted * jnp.transpose(rescale, (2, 0, 1))[..., None] + jnp.einsum(
            "gaqk,kge->qgae",
            weight.astype(jnp.bfloat16),
            value_block,
            preferred_element_type=jnp.float32,
        )
        return ((new_max, row_sum, weighted), None)

    start_state = (
        jnp.full((kv_local, per_group, shard_len), -jnp.inf, jnp.float32),
        jnp.zeros((kv_local, per_group, shard_len), jnp.float32),
        jnp.zeros((shard_len, kv_local, per_group, head_dim), jnp.float32),
    )
    final_state = lax.scan(online_step, start_state, (block_ids, keys_all, values_all))[0]
    row_sum, weighted = (final_state[1], final_state[2])
    attended = (
        (weighted / jnp.transpose(row_sum, (2, 0, 1))[..., None])
        .reshape(shard_len, kv_local * per_group, head_dim)
        .astype(jnp.bfloat16)
    )
    target = lax.psum_scatter(
        jnp.einsum("the,hec->ct", attended, distill_proj, preferred_element_type=jnp.float32),
        ("role", "head"),
        scatter_dimension=0,
        tiled=True,
    )
    signal = conv_input.astype(jnp.float32)
    gate_part = gate_input.astype(jnp.float32)
    full_len = 2 * devices * shard_len
    seq_total = devices * shard_len
    freq_all = jnp.arange(2 * devices, dtype=jnp.int32)
    time_all = jnp.arange(shard_len, dtype=jnp.int32)
    part_len = shard_len // devices
    freq_mine = 2 * seq_rank + jnp.arange(2, dtype=jnp.int32)
    time_mine = seq_rank * part_len + jnp.arange(part_len, dtype=jnp.int32)

    def to_rows(stacked):
        return lax.all_to_all(stacked, "seq", split_axis=3, concat_axis=2, tiled=True)

    def to_cols(stacked):
        return lax.all_to_all(stacked, "seq", split_axis=2, concat_axis=3, tiled=True)

    def forward(stacked):
        pieces = stacked.shape[0]
        arrived = to_rows(stacked[:, :, None, :])
        real_part, imag_part = spread_rows(arrived)
        real_part, imag_part = twist(real_part, imag_part, freq_all, time_mine, full_len, -1.0)
        joined = to_cols(jnp.concatenate([real_part, imag_part], axis=0))
        return along_block(joined[:pieces], joined[pieces:], -1.0)

    def inverse(real_part, imag_part):
        pieces = real_part.shape[0]
        real_part, imag_part = along_block(real_part, imag_part, 1.0)
        real_part, imag_part = twist(real_part, imag_part, freq_mine, time_all, full_len, 1.0)
        arrived = to_rows(jnp.concatenate([real_part, imag_part], axis=0))
        rebuilt = gather_rows(arrived[:pieces], arrived[pieces:], full_len)
        return to_cols(rebuilt)[:, :, 0, :]

    grad_input, filter_step = student(
        signal, gate_part, filter_taps, target, skip_gain, forward, inverse, seq_total
    )
    return (grad_input, filter_step)


def half_step_table(length):
    product = np.arange(length)[:, None] * (2 * np.arange(length)[None, :] + 1) % (4 * length)
    angle = product * (math.pi / (2 * length))
    whole = np.concatenate([np.cos(angle), np.sin(angle)], axis=1)
    upper = whole.astype(ml_dtypes.bfloat16)
    lower = (whole - upper.astype(np.float64)).astype(ml_dtypes.bfloat16)
    return np.stack([upper, lower])


def fits_fused(query_heads, key_heads, value_heads, distill_proj, conv_input, gate_input, filter_taps, skip_gain):
    seq_total = lax.axis_size("seq") * query_heads.shape[0]
    groups = lax.axis_size("role") * lax.axis_size("head")
    chan_local = conv_input.shape[0]
    return (
        seq_total <= min(WINDOW, 1024)
        and query_heads.shape[0] % 128 == 0
        and key_heads.shape[1] == 1
        and key_heads.shape[2] % 128 == 0
        and chan_local % 128 == 0
        and chan_local * groups == distill_proj.shape[2]
    )


def dot_nt(left, right):
    return lax.dot_general(left, right, (((1,), (1,)), ((), ())), preferred_element_type=jnp.float32)


def forward(rows, table_buf, where):
    upper = jnp.dot(rows, table_buf[0, where, :], preferred_element_type=jnp.float32)
    return upper + jnp.dot(rows, table_buf[1, where, :], preferred_element_type=jnp.float32)


def inverse(spec, turned_buf):
    upper = spec.astype(jnp.bfloat16)
    lower = (spec - upper.astype(jnp.float32)).astype(jnp.bfloat16)
    both = jnp.concatenate([upper, lower], axis=0)
    first = jnp.dot(both, turned_buf[0], preferred_element_type=jnp.float32)
    second = jnp.dot(upper, turned_buf[1], preferred_element_type=jnp.float32)
    return first[: spec.shape[0]] + (first[spec.shape[0]:] + second)


def fused_kernel(
    seq_n, role_n, head_n, heads,
    query_hbm, key_hbm, value_hbm, proj_hbm, signal_hbm, gate_hbm, taps_hbm, skip_hbm, table_hbm, turned_hbm,
    grad_ref, step_ref,
    query_buf, key_buf, value_buf, proj_buf, gate_buf, taps_buf, skip_buf, table_buf, turned_buf,
    pair_buf, spec_buf, out_buf, part_send, part_recv, back_buf,
    local_sem, gather_send, gather_recv, part_send_sem, part_recv_sem, back_send, back_recv,
):
    group_n = role_n * head_n
    mine = lax.axis_index("seq")
    group = lax.axis_index("role") * head_n + lax.axis_index("head")
    span = key_hbm.shape[0]
    chans = gate_buf.shape[0]
    seq_total = seq_n * span
    head_dim = key_hbm.shape[1]
    here = pl.ds(pl.multiple_of(mine * span, span), span)

    def place(rank):
        return pl.ds(pl.multiple_of(rank * span, span), span)

    def seq_peer(step):
        return lax.rem(mine + step, seq_n)

    def seq_from(step):
        return lax.rem(mine + seq_n - step, seq_n)

    def group_peer(step):
        other = lax.rem(group + step, group_n)
        return other, {"role": other // head_n, "head": lax.rem(other, head_n)}

    def group_from(step):
        return lax.rem(group + group_n - step, group_n)

    signal_rows, taps_rows = pl.ds(0, chans), pl.ds(chans, chans)
    locals_ = [
        pltpu.make_async_copy(source, target, local_sem.at[index])
        for index, (source, target) in enumerate([
            (taps_hbm, taps_buf),
            (query_hbm, query_buf),
            (key_hbm, key_buf.at[here]),
            (value_hbm, value_buf.at[here]),
            (signal_hbm, pair_buf.at[signal_rows, here]),
            (proj_hbm, proj_buf),
            (gate_hbm, gate_buf),
            (skip_hbm, skip_buf),
            (table_hbm, table_buf),
            (turned_hbm.at[:, :, here], turned_buf),
        ])
    ]
    for copy in locals_:
        copy.start()
    taps_copy, query_copy, key_copy, value_copy, signal_copy, proj_copy, gate_copy, skip_copy, table_copy, turned_copy = locals_

    barrier = pltpu.get_barrier_semaphore()
    for step in range(1, seq_n):
        pl.semaphore_signal(barrier, inc=1, device_id={"seq": seq_peer(step)}, device_id_type=MESH)
    for step in range(1, group_n):
        pl.semaphore_signal(barrier, inc=1, device_id=group_peer(step)[1], device_id_type=MESH)
    taps_copy.wait()
    pair_buf[taps_rows, here] = taps_buf[...].astype(jnp.bfloat16)
    rows = query_buf.shape[0]
    row_id = lax.broadcasted_iota(jnp.int32, (rows, rows), 0)
    col_id = lax.broadcasted_iota(jnp.int32, (rows, rows), 1)
    wanted = (row_id % span) * heads + row_id // span
    order = jnp.where(col_id == wanted, 1.0, 0.0).astype(jnp.bfloat16)
    query_copy.wait()
    queries = jnp.dot(order, query_buf[...], preferred_element_type=jnp.float32).astype(jnp.bfloat16)
    pl.semaphore_wait(barrier, seq_n + group_n - 2)

    gathered = (
        lambda owner: key_buf.at[place(owner)],
        lambda owner: value_buf.at[place(owner)],
        lambda owner: pair_buf.at[signal_rows, place(owner)],
        lambda owner: pair_buf.at[taps_rows, place(owner)],
    )
    sources = (key_hbm, value_hbm, signal_hbm, pair_buf.at[taps_rows, here])

    def gather(kind, step, owner):
        return pltpu.make_async_remote_copy(
            src_ref=sources[kind],
            dst_ref=gathered[kind](owner),
            send_sem=gather_send.at[kind, step],
            recv_sem=gather_recv.at[kind, owner],
            device_id={"seq": seq_peer(step)},
            device_id_type=MESH,
        )

    far_first = sorted(range(1, seq_n), key=lambda step: abs(2 * step - seq_n))
    sends = []

    def send_gather(kind):
        for step in far_first:
            copy = gather(kind, step, mine)
            copy.start()
            sends.append(copy)

    width = 2 if seq_n % 2 == 0 else 1

    def chunk(step):
        first = lax.rem(mine // width + step, seq_n // width) * width
        if step:
            owners = [first + inner for inner in range(width)]
        else:
            owners = [first + lax.rem(mine + 1, 2)] if width == 2 else []
        return first, owners, pl.ds(pl.multiple_of(first * span, width * span), width * span)

    send_gather(0)
    send_gather(1)
    key_copy.wait()
    value_copy.wait()
    for step in range(seq_n // width):
        first, owners, where = chunk(step)
        for owner in owners:
            gather(0, 1, owner).wait_recv()
        scores = dot_nt(queries, key_buf[where, :]) * (head_dim ** -0.5)
        query_pos = mine * span + lax.broadcasted_iota(jnp.int32, scores.shape, 0) % span
        key_pos = first * span + lax.broadcasted_iota(jnp.int32, scores.shape, 1)
        live = key_pos <= query_pos
        scores = jnp.where(live, scores, -jnp.inf)
        chunk_max = jnp.max(scores, axis=1, keepdims=True)
        new_max = jnp.maximum(row_max, chunk_max) if step else chunk_max
        weight = jnp.exp(scores - new_max)
        chunk_sum = jnp.sum(weight, axis=1, keepdims=True)
        for owner in owners:
            gather(1, 1, owner).wait_recv()
        if step == seq_n // width - 1:
            send_gather(2)
            send_gather(3)
        product = jnp.dot(weight.astype(jnp.bfloat16), value_buf[where, :], preferred_element_type=jnp.float32)
        if step:
            rescale = jnp.exp(row_max - new_max)
            row_sum = row_sum * rescale + chunk_sum
            weighted = weighted * rescale + product
        else:
            row_sum, weighted = chunk_sum, product
        row_max = new_max
    attended = (weighted / row_sum).astype(jnp.bfloat16)

    proj_copy.wait()
    def part_copy(other, slot):
        return pltpu.make_async_remote_copy(
            src_ref=part_send.at[other],
            dst_ref=part_recv.at[slot],
            send_sem=part_send_sem.at[other],
            recv_sem=part_recv_sem.at[slot],
            device_id={"role": other // head_n, "head": lax.rem(other, head_n)},
            device_id_type=MESH,
        )

    couple = 2 if group_n % 2 == 0 else 1
    for step in list(range(1, group_n // couple)) + [0]:
        first = lax.rem(group // couple + step, group_n // couple) * couple
        columns = pl.ds(pl.multiple_of(first * chans, couple * chans), couple * chans)
        partial = 0.0
        for head in range(heads):
            partial = partial + jnp.dot(
                attended[head * span:(head + 1) * span],
                proj_buf[head, :, columns],
                preferred_element_type=jnp.float32,
            )
        for inner in range(couple):
            part_send[first + inner] = partial[:, inner * chans:(inner + 1) * chans].astype(jnp.bfloat16)
        if step:
            others = [first + inner for inner in range(couple)]
        else:
            others = [first + lax.rem(group + 1, 2)] if couple == 2 else []
        for other in others:
            copy = part_copy(other, group)
            copy.start()
            sends.append(copy)

    signal_copy.wait()
    for step in range(1, seq_n):
        gather(2, step, seq_from(step)).wait_recv()
        gather(3, step, seq_from(step)).wait_recv()
    table_copy.wait()
    turned_copy.wait()
    gate_copy.wait()
    skip_copy.wait()
    spec_buf[...] = forward(pair_buf[...], table_buf, slice(None))
    low, high = pl.ds(0, seq_total), pl.ds(seq_total, seq_total)
    input_c, input_s = spec_buf[signal_rows, low], spec_buf[signal_rows, high]
    taps_c, taps_s = spec_buf[taps_rows, low], spec_buf[taps_rows, high]
    conv_spec = jnp.concatenate(
        [input_c * taps_c - input_s * taps_s, input_c * taps_s + input_s * taps_c], axis=1
    )
    conv = inverse(conv_spec, turned_buf) * (1.0 / seq_total)
    skip = jnp.transpose(jnp.broadcast_to(skip_buf[...], (span, chans)))
    gate = gate_buf[...].astype(jnp.float32)
    out_buf[...] = gate * (conv + skip * pair_buf[signal_rows, here].astype(jnp.float32))

    target = part_send[group].astype(jnp.float32)
    for step in range(1, group_n):
        source = group_from(step)
        part_copy(source, source).wait_recv()
        target = target + part_recv[source].astype(jnp.float32)
    back = gate * (out_buf[...] - jnp.transpose(target))
    back_buf[:, here] = back.astype(jnp.bfloat16)

    def back_copy(step, owner):
        where = place(owner)
        return pltpu.make_async_remote_copy(
            src_ref=back_buf.at[:, here],
            dst_ref=back_buf.at[:, where],
            send_sem=back_send.at[step],
            recv_sem=back_recv.at[owner],
            device_id={"seq": seq_peer(step)},
            device_id_type=MESH,
        )

    for step in far_first:
        copy = back_copy(step, mine)
        copy.start()
        sends.append(copy)
    back_spec = 0.0
    for step in range(seq_n // width):
        _, owners, where = chunk(step)
        for owner in owners:
            back_copy(1, owner).wait_recv()
        back_spec = back_spec + forward(back_buf[:, where], table_buf, where)
    back_c, back_s = back_spec[:, :seq_total], back_spec[:, seq_total:]

    def correlation(rows):
        first_c, first_s = spec_buf[rows, low], spec_buf[rows, high]
        return jnp.concatenate([first_c * back_c + first_s * back_s, first_c * back_s - first_s * back_c], axis=1)

    lags = inverse(jnp.concatenate([correlation(taps_rows), correlation(signal_rows)], axis=0), turned_buf)
    grad_ref[...] = skip * back + lags[:chans] * (1.0 / seq_total)
    step_ref[...] = lags[chans:] * (seq_total ** -1.5)
    for copy in sends:
        copy.wait_send()


def hand_over(grad_in, step_in, grad_out, step_out, sems):
    copies = [
        pltpu.make_async_copy(grad_in, grad_out, sems.at[0]),
        pltpu.make_async_copy(step_in, step_out, sems.at[1]),
    ]
    for copy in copies:
        copy.start()
    for copy in copies:
        copy.wait()


def fused_body(query_heads, key_heads, value_heads, distill_proj, conv_input, gate_input, filter_taps, skip_gain):
    span, heads, head_dim = query_heads.shape
    seq_n, role_n, head_n = (lax.axis_size(axis) for axis in ("seq", "role", "head"))
    group_n = role_n * head_n
    seq_total = seq_n * span
    chans = conv_input.shape[0]
    table_terms = half_step_table(seq_total)
    table = jnp.asarray(table_terms)
    turned = jnp.asarray(np.ascontiguousarray(np.swapaxes(table_terms, 1, 2)))
    in_hbm = pl.BlockSpec(memory_space=pltpu.HBM)
    vmem = pl.BlockSpec(memory_space=pltpu.VMEM)
    bf16, f32 = jnp.bfloat16, jnp.float32
    dma = pltpu.SemaphoreType.DMA
    results = pl.pallas_call(
        functools.partial(fused_kernel, seq_n, role_n, head_n, heads),
        out_shape=[jax.ShapeDtypeStruct((chans, span), f32)] * 2,
        in_specs=[in_hbm] * 10,
        out_specs=[vmem, vmem],
        scratch_shapes=[
            pltpu.VMEM((span * heads, head_dim), bf16),
            pltpu.VMEM((seq_total, head_dim), bf16),
            pltpu.VMEM((seq_total, head_dim), bf16),
            pltpu.VMEM(distill_proj.shape, bf16),
            pltpu.VMEM((chans, span), bf16),
            pltpu.VMEM((chans, span), f32),
            pltpu.VMEM((1, chans), f32),
            pltpu.VMEM(table.shape, bf16),
            pltpu.VMEM((2, 2 * seq_total, span), bf16),
            pltpu.VMEM((2 * chans, seq_total), bf16),
            pltpu.VMEM((2 * chans, 2 * seq_total), f32),
            pltpu.VMEM((chans, span), f32),
            pltpu.VMEM((group_n, span, chans), bf16),
            pltpu.VMEM((group_n, span, chans), bf16),
            pltpu.VMEM((chans, seq_total), bf16),
            dma((10,)),
            dma((4, seq_n)),
            dma((4, seq_n)),
            dma((group_n,)),
            dma((group_n,)),
            dma((seq_n,)),
            dma((seq_n,)),
        ],
        compiler_params=pltpu.CompilerParams(
            collective_id=0, has_side_effects=True, vmem_limit_bytes=63 * 1024 * 1024
        ),
    )(
        query_heads.reshape(span * heads, head_dim),
        key_heads.reshape(span, head_dim),
        value_heads.reshape(span, head_dim),
        distill_proj,
        conv_input,
        gate_input,
        filter_taps,
        skip_gain.reshape(1, chans),
        table,
        turned,
    )
    return pl.pallas_call(
        hand_over,
        out_shape=[jax.ShapeDtypeStruct((chans, span), f32)] * 2,
        in_specs=[in_hbm] * 2,
        out_specs=[in_hbm] * 2,
        scratch_shapes=[dma((2,))],
        compiler_params=pltpu.CompilerParams(vmem_limit_bytes=63 * 1024 * 1024),
    )(*results)


def solution(mesh):
    in_specs = (
        P("seq", ("role", "head"), None),
        P("seq", ("role", "head"), None),
        P("seq", ("role", "head"), None),
        P(("role", "head"), None, None),
        P(("role", "head"), "seq"),
        P(("role", "head"), "seq"),
        P(("role", "head"), "seq"),
        P(("role", "head")),
    )
    out_specs = (P(("role", "head"), "seq"), P(("role", "head"), "seq"))
    def chosen(*arrays):
        return fused_body(*arrays) if fits_fused(*arrays) else body(*arrays)

    return jax.shard_map(chosen, mesh=mesh, in_specs=in_specs, out_specs=out_specs, check_vma=False)
```

```python
import functools
import math

import jax
import jax.numpy as jnp
import ml_dtypes
import numpy as np
from jax import lax
from jax.experimental import pallas as pl
from jax.experimental.pallas import tpu as pltpu
from jax.sharding import PartitionSpec as P

WINDOW = 4096
MESH = pl.DeviceIdType.MESH
highest = lax.Precision.HIGHEST


def shifted(value, axis, steps):
    count = lax.axis_size(axis)
    leading, last = (max(0, -steps), min(count, count - steps))
    return lax.ppermute(value, axis, [(source, source + steps) for source in range(leading, last)])


def angle_table(row_ids, col_ids, length):
    product = row_ids[:, None] * col_ids[None, :] % length
    quarter = length // 4
    eighth = length // 8
    quadrant = product // quarter
    within = product % quarter
    flipped = within > eighth
    reduced = jnp.where(flipped, quarter - within, within)
    angles = reduced.astype(jnp.float32) * (2.0 * math.pi / length)
    base_cos = jnp.cos(angles)
    base_sin = jnp.sin(angles)
    first_cos = jnp.where(flipped, base_sin, base_cos)
    first_sin = jnp.where(flipped, base_cos, base_sin)
    cosine = jnp.where(
        quadrant == 0,
        first_cos,
        jnp.where(quadrant == 1, -first_sin, jnp.where(quadrant == 2, -first_cos, first_sin)),
    )
    sine_part = jnp.where(
        quadrant == 0,
        first_sin,
        jnp.where(quadrant == 1, first_cos, jnp.where(quadrant == 2, -first_sin, -first_cos)),
    )
    return (cosine, sine_part)


def spread_rows(stacked):
    pieces = stacked.shape[2]
    cosine, sine_part = angle_table(
        jnp.arange(2 * pieces, dtype=jnp.int32), jnp.arange(pieces, dtype=jnp.int32), 2 * pieces
    )
    real_part = jnp.einsum("kd,ncdr->nckr", cosine, stacked, precision=highest)
    imag_part = -jnp.einsum("kd,ncdr->nckr", sine_part, stacked, precision=highest)
    return (real_part, imag_part)


def twist(real_part, imag_part, freq_ids, time_ids, length, turning):
    cosine, sine_part = angle_table(freq_ids, time_ids, length)
    return (
        real_part * cosine - turning * imag_part * sine_part,
        imag_part * cosine + turning * real_part * sine_part,
    )


def along_block(real_part, imag_part, turning):
    length = real_part.shape[-1]
    cosine, sine_part = angle_table(
        jnp.arange(length, dtype=jnp.int32), jnp.arange(length, dtype=jnp.int32), length
    )
    out_real = jnp.einsum(
        "nckb,bj->nckj", real_part, cosine, precision=highest
    ) - turning * jnp.einsum("nckb,bj->nckj", imag_part, sine_part, precision=highest)
    out_imag = jnp.einsum(
        "nckb,bj->nckj", imag_part, cosine, precision=highest
    ) + turning * jnp.einsum("nckb,bj->nckj", real_part, sine_part, precision=highest)
    return (out_real, out_imag)


def gather_rows(real_part, imag_part, length):
    doubled = real_part.shape[2]
    cosine, sine_part = angle_table(
        jnp.arange(doubled // 2, dtype=jnp.int32), jnp.arange(doubled, dtype=jnp.int32), doubled
    )
    signal = jnp.einsum("dk,nckr->ncdr", cosine, real_part, precision=highest) - jnp.einsum(
        "dk,nckr->ncdr", sine_part, imag_part, precision=highest
    )
    return signal / length


def student(signal, gate_part, taps, target, skip_part, forward, inverse, seq_total):
    spec_real, spec_imag = forward(jnp.stack([signal, taps]))
    input_re, taps_re = (spec_real[0], spec_real[1])
    input_im, taps_im = (spec_imag[0], spec_imag[1])
    conv_re = input_re * taps_re - input_im * taps_im
    conv_im = input_re * taps_im + input_im * taps_re
    convolved = inverse(conv_re[None], conv_im[None])[0]
    output = gate_part * (convolved + skip_part[:, None] * signal)
    backed = gate_part * (output - target)
    back_real, back_imag = forward(backed[None])
    back_re, back_im = (back_real[0], back_imag[0])
    left_re = taps_re * back_re + taps_im * back_im
    left_im = taps_re * back_im - taps_im * back_re
    right_re = input_re * back_re + input_im * back_im
    right_im = input_re * back_im - input_im * back_re
    corrected = inverse(jnp.stack([left_re, right_re]), jnp.stack([left_im, right_im]))
    grad_input = skip_part[:, None] * backed + corrected[0]
    filter_step = corrected[1] * seq_total ** (-0.5)
    return (grad_input, filter_step)


def body(
    query_heads,
    key_heads,
    value_heads,
    distill_proj,
    conv_input,
    gate_input,
    filter_taps,
    skip_gain,
):
    shard_len = query_heads.shape[0]
    kv_local = key_heads.shape[1]
    per_group = query_heads.shape[1] // kv_local
    head_dim = query_heads.shape[2]
    devices = lax.axis_size("seq")
    seq_rank = lax.axis_index("seq")
    shards = min((WINDOW + shard_len - 1) // shard_len, devices - 1)
    per_step = max(1, 512 // shard_len)
    total_shards = -(-(shards + 1) // per_step) * per_step
    own_block = jnp.stack([key_heads, value_heads])
    buffer = jnp.concatenate(
        [jnp.zeros((total_shards - 1,) + own_block.shape, jnp.bfloat16), own_block[None]], axis=0
    )

    def fetch(step_id, carried):
        current, stored = carried
        current = shifted(current, "seq", 1)
        stored = lax.dynamic_update_index_in_dim(stored, current, total_shards - 1 - step_id, 0)
        return (current, stored)

    buffer = lax.fori_loop(1, shards + 1, fetch, (own_block, buffer))[1]
    key_span = per_step * shard_len
    blocks = total_shards // per_step
    keys_all = buffer[:, 0].reshape(blocks, key_span, kv_local, head_dim)
    values_all = buffer[:, 1].reshape(blocks, key_span, kv_local, head_dim)
    first_key = (seq_rank + 1 - total_shards) * shard_len
    query_pos = seq_rank * shard_len + jnp.arange(shard_len, dtype=jnp.int32)
    queries = query_heads.reshape(shard_len, kv_local, per_group, head_dim)
    score_scale = head_dim ** (-0.5)
    block_ids = jnp.arange(blocks, dtype=jnp.int32)

    def online_step(carried, element):
        row_max, row_sum, weighted = carried
        block_id, key_block, value_block = element
        scores = (
            jnp.einsum("qgae,kge->gaqk", queries, key_block, preferred_element_type=jnp.float32)
            * score_scale
        )
        key_pos = first_key + block_id * key_span + jnp.arange(key_span, dtype=jnp.int32)
        in_window = (
            (key_pos[None, :] <= query_pos[:, None])
            & (key_pos[None, :] > query_pos[:, None] - WINDOW)
            & (key_pos[None, :] >= 0)
        )
        new_max = jnp.maximum(row_max, jnp.max(jnp.where(in_window, scores, -jnp.inf), axis=-1))
        safe_max = jnp.where(new_max == -jnp.inf, 0.0, new_max)
        rescale = jnp.exp(row_max - safe_max)
        weight = jnp.where(in_window, jnp.exp(scores - safe_max[..., None]), 0.0)
        row_sum = row_sum * rescale + jnp.sum(weight, axis=-1)
        weighted = weighted * jnp.transpose(rescale, (2, 0, 1))[..., None] + jnp.einsum(
            "gaqk,kge->qgae",
            weight.astype(jnp.bfloat16),
            value_block,
            preferred_element_type=jnp.float32,
        )
        return ((new_max, row_sum, weighted), None)

    start_state = (
        jnp.full((kv_local, per_group, shard_len), -jnp.inf, jnp.float32),
        jnp.zeros((kv_local, per_group, shard_len), jnp.float32),
        jnp.zeros((shard_len, kv_local, per_group, head_dim), jnp.float32),
    )
    final_state = lax.scan(online_step, start_state, (block_ids, keys_all, values_all))[0]
    row_sum, weighted = (final_state[1], final_state[2])
    attended = (
        (weighted / jnp.transpose(row_sum, (2, 0, 1))[..., None])
        .reshape(shard_len, kv_local * per_group, head_dim)
        .astype(jnp.bfloat16)
    )
    target = lax.psum_scatter(
        jnp.einsum("the,hec->ct", attended, distill_proj, preferred_element_type=jnp.float32),
        ("role", "head"),
        scatter_dimension=0,
        tiled=True,
    )
    signal = conv_input.astype(jnp.float32)
    gate_part = gate_input.astype(jnp.float32)
    full_len = 2 * devices * shard_len
    seq_total = devices * shard_len
    freq_all = jnp.arange(2 * devices, dtype=jnp.int32)
    time_all = jnp.arange(shard_len, dtype=jnp.int32)
    part_len = shard_len // devices
    freq_mine = 2 * seq_rank + jnp.arange(2, dtype=jnp.int32)
    time_mine = seq_rank * part_len + jnp.arange(part_len, dtype=jnp.int32)

    def to_rows(stacked):
        return lax.all_to_all(stacked, "seq", split_axis=3, concat_axis=2, tiled=True)

    def to_cols(stacked):
        return lax.all_to_all(stacked, "seq", split_axis=2, concat_axis=3, tiled=True)

    def forward(stacked):
        pieces = stacked.shape[0]
        arrived = to_rows(stacked[:, :, None, :])
        real_part, imag_part = spread_rows(arrived)
        real_part, imag_part = twist(real_part, imag_part, freq_all, time_mine, full_len, -1.0)
        joined = to_cols(jnp.concatenate([real_part, imag_part], axis=0))
        return along_block(joined[:pieces], joined[pieces:], -1.0)

    def inverse(real_part, imag_part):
        pieces = real_part.shape[0]
        real_part, imag_part = along_block(real_part, imag_part, 1.0)
        real_part, imag_part = twist(real_part, imag_part, freq_mine, time_all, full_len, 1.0)
        arrived = to_rows(jnp.concatenate([real_part, imag_part], axis=0))
        rebuilt = gather_rows(arrived[:pieces], arrived[pieces:], full_len)
        return to_cols(rebuilt)[:, :, 0, :]

    grad_input, filter_step = student(
        signal, gate_part, filter_taps, target, skip_gain, forward, inverse, seq_total
    )
    return (grad_input, filter_step)


def half_step_table(length):
    product = np.arange(length)[:, None] * (2 * np.arange(length)[None, :] + 1) % (4 * length)
    angle = product * (math.pi / (2 * length))
    whole = np.concatenate([np.cos(angle), np.sin(angle)], axis=1)
    upper = whole.astype(ml_dtypes.bfloat16)
    lower = (whole - upper.astype(np.float64)).astype(ml_dtypes.bfloat16)
    return np.stack([upper, lower])


def fits_fused(query_heads, key_heads, value_heads, distill_proj, conv_input, gate_input, filter_taps, skip_gain):
    seq_total = lax.axis_size("seq") * query_heads.shape[0]
    groups = lax.axis_size("role") * lax.axis_size("head")
    chan_local = conv_input.shape[0]
    return (
        seq_total <= min(WINDOW, 1024)
        and query_heads.shape[0] % 128 == 0
        and key_heads.shape[1] == 1
        and key_heads.shape[2] % 128 == 0
        and chan_local % 128 == 0
        and chan_local * groups == distill_proj.shape[2]
    )


def dot_nt(left, right):
    return lax.dot_general(left, right, (((1,), (1,)), ((), ())), preferred_element_type=jnp.float32)


def forward(rows, table_buf, where):
    upper = jnp.dot(rows, table_buf[0, where, :], preferred_element_type=jnp.float32)
    return upper + jnp.dot(rows, table_buf[1, where, :], preferred_element_type=jnp.float32)


def inverse(spec, turned_buf):
    upper = spec.astype(jnp.bfloat16)
    lower = (spec - upper.astype(jnp.float32)).astype(jnp.bfloat16)
    width = turned_buf.shape[1] // 2
    wide = jnp.dot(upper, turned_buf[...], preferred_element_type=jnp.float32)
    rest = jnp.dot(lower, turned_buf[:, :width], preferred_element_type=jnp.float32)
    return wide[:, :width] + (wide[:, width:] + rest)


def fused_kernel(
    seq_n, role_n, head_n, heads,
    query_hbm, key_hbm, value_hbm, proj_hbm, signal_hbm, gate_hbm, taps_hbm, skip_hbm, table_hbm, turned_hbm,
    grad_ref, step_ref,
    query_buf, key_buf, value_buf, proj_buf, gate_buf, taps_buf, skip_buf, table_buf, turned_buf,
    pair_buf, spec_buf, out_buf, part_send, part_recv, back_buf,
    local_sem, gather_send, gather_recv, part_send_sem, part_recv_sem, back_send, back_recv,
):
    group_n = role_n * head_n
    mine = lax.axis_index("seq")
    group = lax.axis_index("role") * head_n + lax.axis_index("head")
    span = key_hbm.shape[0]
    chans = gate_buf.shape[0]
    seq_total = seq_n * span
    head_dim = key_hbm.shape[1]
    here = pl.ds(pl.multiple_of(mine * span, span), span)

    def place(rank):
        return pl.ds(pl.multiple_of(rank * span, span), span)

    def seq_peer(step):
        return lax.rem(mine + step, seq_n)

    def seq_from(step):
        return lax.rem(mine + seq_n - step, seq_n)

    def group_peer(step):
        other = lax.rem(group + step, group_n)
        return other, {"role": other // head_n, "head": lax.rem(other, head_n)}

    def group_from(step):
        return lax.rem(group + group_n - step, group_n)

    signal_rows, taps_rows = pl.ds(0, chans), pl.ds(chans, chans)
    locals_ = [
        pltpu.make_async_copy(source, target, local_sem.at[index])
        for index, (source, target) in enumerate([
            (taps_hbm, taps_buf),
            (query_hbm, query_buf),
            (key_hbm, key_buf.at[here]),
            (value_hbm, value_buf.at[here]),
            (signal_hbm, pair_buf.at[signal_rows, here]),
            (proj_hbm, proj_buf),
            (gate_hbm, gate_buf),
            (skip_hbm, skip_buf),
            (table_hbm, table_buf),
            (turned_hbm.at[:, pl.ds(pl.multiple_of(2 * mine * span, 2 * span), 2 * span)], turned_buf),
        ])
    ]
    for copy in locals_:
        copy.start()
    taps_copy, query_copy, key_copy, value_copy, signal_copy, proj_copy, gate_copy, skip_copy, table_copy, turned_copy = locals_

    barrier = pltpu.get_barrier_semaphore()
    for step in range(1, seq_n):
        pl.semaphore_signal(barrier, inc=1, device_id={"seq": seq_peer(step)}, device_id_type=MESH)
    for step in range(1, group_n):
        pl.semaphore_signal(barrier, inc=1, device_id=group_peer(step)[1], device_id_type=MESH)
    taps_copy.wait()
    pair_buf[taps_rows, here] = taps_buf[...].astype(jnp.bfloat16)
    rows = query_buf.shape[0]
    row_id = lax.broadcasted_iota(jnp.int32, (rows, rows), 0)
    col_id = lax.broadcasted_iota(jnp.int32, (rows, rows), 1)
    wanted = (row_id % span) * heads + row_id // span
    order = jnp.where(col_id == wanted, 1.0, 0.0).astype(jnp.bfloat16)
    query_copy.wait()
    queries = jnp.dot(order, query_buf[...], preferred_element_type=jnp.float32).astype(jnp.bfloat16)
    pl.semaphore_wait(barrier, seq_n + group_n - 2)

    gathered = (
        lambda owner: key_buf.at[place(owner)],
        lambda owner: value_buf.at[place(owner)],
        lambda owner: pair_buf.at[signal_rows, place(owner)],
        lambda owner: pair_buf.at[taps_rows, place(owner)],
    )
    sources = (key_hbm, value_hbm, signal_hbm, pair_buf.at[taps_rows, here])

    def gather(kind, step, owner):
        return pltpu.make_async_remote_copy(
            src_ref=sources[kind],
            dst_ref=gathered[kind](owner),
            send_sem=gather_send.at[kind, step],
            recv_sem=gather_recv.at[kind, owner],
            device_id={"seq": seq_peer(step)},
            device_id_type=MESH,
        )

    far_first = sorted(range(1, seq_n), key=lambda step: abs(2 * step - seq_n))
    sends = []

    def send_gather(kind):
        for step in far_first:
            copy = gather(kind, step, mine)
            copy.start()
            sends.append(copy)

    width = 2 if seq_n % 2 == 0 else 1

    def chunk(step):
        first = lax.rem(mine // width + step, seq_n // width) * width
        if step:
            owners = [first + inner for inner in range(width)]
        else:
            owners = [first + lax.rem(mine + 1, 2)] if width == 2 else []
        return first, owners, pl.ds(pl.multiple_of(first * span, width * span), width * span)

    send_gather(0)
    send_gather(1)
    key_copy.wait()
    value_copy.wait()
    for step in range(seq_n // width):
        first, owners, where = chunk(step)
        for owner in owners:
            gather(0, 1, owner).wait_recv()
        scores = dot_nt(queries, key_buf[where, :]) * (head_dim ** -0.5)
        query_pos = mine * span + lax.broadcasted_iota(jnp.int32, scores.shape, 0) % span
        key_pos = first * span + lax.broadcasted_iota(jnp.int32, scores.shape, 1)
        live = key_pos <= query_pos
        scores = jnp.where(live, scores, -jnp.inf)
        chunk_max = jnp.max(scores, axis=1, keepdims=True)
        new_max = jnp.maximum(row_max, chunk_max) if step else chunk_max
        weight = jnp.exp(scores - new_max)
        chunk_sum = jnp.sum(weight, axis=1, keepdims=True)
        for owner in owners:
            gather(1, 1, owner).wait_recv()
        if step == seq_n // width - 1:
            send_gather(2)
            send_gather(3)
        product = jnp.dot(weight.astype(jnp.bfloat16), value_buf[where, :], preferred_element_type=jnp.float32)
        if step:
            rescale = jnp.exp(row_max - new_max)
            row_sum = row_sum * rescale + chunk_sum
            weighted = weighted * rescale + product
        else:
            row_sum, weighted = chunk_sum, product
        row_max = new_max
    attended = (weighted / row_sum).astype(jnp.bfloat16)

    proj_copy.wait()
    def part_copy(other, slot):
        return pltpu.make_async_remote_copy(
            src_ref=part_send.at[other],
            dst_ref=part_recv.at[slot],
            send_sem=part_send_sem.at[other],
            recv_sem=part_recv_sem.at[slot],
            device_id={"role": other // head_n, "head": lax.rem(other, head_n)},
            device_id_type=MESH,
        )

    couple = 2 if group_n % 2 == 0 else 1
    for step in list(range(1, group_n // couple, 2)) + list(range(2, group_n // couple, 2)) + [0]:
        first = lax.rem(group // couple + step, group_n // couple) * couple
        columns = pl.ds(pl.multiple_of(first * chans, couple * chans), couple * chans)
        partial = 0.0
        for head in range(heads):
            partial = partial + jnp.dot(
                attended[head * span:(head + 1) * span],
                proj_buf[head, :, columns],
                preferred_element_type=jnp.float32,
            )
        for inner in range(couple):
            part_send[first + inner] = partial[:, inner * chans:(inner + 1) * chans].astype(jnp.bfloat16)
        if step:
            others = [first + inner for inner in range(couple)]
        else:
            others = [first + lax.rem(group + 1, 2)] if couple == 2 else []
        for other in others:
            copy = part_copy(other, group)
            copy.start()
            sends.append(copy)

    signal_copy.wait()
    for step in range(1, seq_n):
        gather(2, step, seq_from(step)).wait_recv()
        gather(3, step, seq_from(step)).wait_recv()
    table_copy.wait()
    turned_copy.wait()
    gate_copy.wait()
    skip_copy.wait()
    spec_buf[...] = forward(pair_buf[...], table_buf, slice(None))
    low, high = pl.ds(0, seq_total), pl.ds(seq_total, seq_total)
    input_c, input_s = spec_buf[signal_rows, low], spec_buf[signal_rows, high]
    taps_c, taps_s = spec_buf[taps_rows, low], spec_buf[taps_rows, high]
    conv_spec = jnp.concatenate(
        [input_c * taps_c - input_s * taps_s, input_c * taps_s + input_s * taps_c], axis=1
    )
    conv = inverse(conv_spec, turned_buf) * (1.0 / seq_total)
    skip = jnp.transpose(jnp.broadcast_to(skip_buf[...], (span, chans)))
    gate = gate_buf[...].astype(jnp.float32)
    out_buf[...] = gate * (conv + skip * pair_buf[signal_rows, here].astype(jnp.float32))

    target = part_send[group].astype(jnp.float32)
    for step in range(1, group_n):
        source = group_from(step)
        part_copy(source, source).wait_recv()
        target = target + part_recv[source].astype(jnp.float32)
    back = gate * (out_buf[...] - jnp.transpose(target))
    back_buf[:, here] = back.astype(jnp.bfloat16)

    def back_copy(step, owner):
        where = place(owner)
        return pltpu.make_async_remote_copy(
            src_ref=back_buf.at[:, here],
            dst_ref=back_buf.at[:, where],
            send_sem=back_send.at[step],
            recv_sem=back_recv.at[owner],
            device_id={"seq": seq_peer(step)},
            device_id_type=MESH,
        )

    for step in far_first:
        copy = back_copy(step, mine)
        copy.start()
        sends.append(copy)
    back_spec = 0.0
    for step in range(seq_n // width):
        _, owners, where = chunk(step)
        for owner in owners:
            back_copy(1, owner).wait_recv()
        back_spec = back_spec + forward(back_buf[:, where], table_buf, where)
    back_c, back_s = back_spec[:, :seq_total], back_spec[:, seq_total:]

    def correlation(rows):
        first_c, first_s = spec_buf[rows, low], spec_buf[rows, high]
        return jnp.concatenate([first_c * back_c + first_s * back_s, first_c * back_s - first_s * back_c], axis=1)

    lags = inverse(jnp.concatenate([correlation(taps_rows), correlation(signal_rows)], axis=0), turned_buf)
    grad_ref[...] = skip * back + lags[:chans] * (1.0 / seq_total)
    step_ref[...] = lags[chans:] * (seq_total ** -1.5)
    for copy in sends:
        copy.wait_send()


def hand_over(grad_in, step_in, grad_out, step_out, held, sems):
    arriving = [
        pltpu.make_async_copy(source, held.at[index], sems.at[index])
        for index, source in enumerate((grad_in, step_in))
    ]
    leaving = [
        pltpu.make_async_copy(held.at[index], target, sems.at[2 + index])
        for index, target in enumerate((grad_out, step_out))
    ]
    for copy in arriving:
        copy.start()
    for first, second in zip(arriving, leaving):
        first.wait()
        second.start()
    for copy in leaving:
        copy.wait()


def fused_body(query_heads, key_heads, value_heads, distill_proj, conv_input, gate_input, filter_taps, skip_gain):
    span, heads, head_dim = query_heads.shape
    seq_n, role_n, head_n = (lax.axis_size(axis) for axis in ("seq", "role", "head"))
    group_n = role_n * head_n
    seq_total = seq_n * span
    chans = conv_input.shape[0]
    table_terms = half_step_table(seq_total)
    table = jnp.asarray(table_terms)
    turned = table_terms.reshape(2, seq_n, span, 2 * seq_total).transpose(3, 1, 0, 2)
    turned = jnp.asarray(np.ascontiguousarray(turned.reshape(2 * seq_total, 2 * seq_total)))
    in_hbm = pl.BlockSpec(memory_space=pltpu.HBM)
    vmem = pl.BlockSpec(memory_space=pltpu.VMEM)
    bf16, f32 = jnp.bfloat16, jnp.float32
    dma = pltpu.SemaphoreType.DMA
    results = pl.pallas_call(
        functools.partial(fused_kernel, seq_n, role_n, head_n, heads),
        out_shape=[jax.ShapeDtypeStruct((chans, span), f32)] * 2,
        in_specs=[in_hbm] * 10,
        out_specs=[vmem, vmem],
        scratch_shapes=[
            pltpu.VMEM((span * heads, head_dim), bf16),
            pltpu.VMEM((seq_total, head_dim), bf16),
            pltpu.VMEM((seq_total, head_dim), bf16),
            pltpu.VMEM(distill_proj.shape, bf16),
            pltpu.VMEM((chans, span), bf16),
            pltpu.VMEM((chans, span), f32),
            pltpu.VMEM((1, chans), f32),
            pltpu.VMEM(table.shape, bf16),
            pltpu.VMEM((2 * seq_total, 2 * span), bf16),
            pltpu.VMEM((2 * chans, seq_total), bf16),
            pltpu.VMEM((2 * chans, 2 * seq_total), f32),
            pltpu.VMEM((chans, span), f32),
            pltpu.VMEM((group_n, span, chans), bf16),
            pltpu.VMEM((group_n, span, chans), bf16),
            pltpu.VMEM((chans, seq_total), bf16),
            dma((10,)),
            dma((4, seq_n)),
            dma((4, seq_n)),
            dma((group_n,)),
            dma((group_n,)),
            dma((seq_n,)),
            dma((seq_n,)),
        ],
        compiler_params=pltpu.CompilerParams(
            collective_id=0, has_side_effects=True, vmem_limit_bytes=63 * 1024 * 1024
        ),
    )(
        query_heads.reshape(span * heads, head_dim),
        key_heads.reshape(span, head_dim),
        value_heads.reshape(span, head_dim),
        distill_proj,
        conv_input,
        gate_input,
        filter_taps,
        skip_gain.reshape(1, chans),
        table,
        turned,
    )
    return pl.pallas_call(
        hand_over,
        out_shape=[jax.ShapeDtypeStruct((chans, span), f32)] * 2,
        in_specs=[in_hbm] * 2,
        out_specs=[in_hbm] * 2,
        scratch_shapes=[pltpu.VMEM((2, chans, span), f32), dma((4,))],
        compiler_params=pltpu.CompilerParams(vmem_limit_bytes=63 * 1024 * 1024),
    )(*results)


def solution(mesh):
    in_specs = (
        P("seq", ("role", "head"), None),
        P("seq", ("role", "head"), None),
        P("seq", ("role", "head"), None),
        P(("role", "head"), None, None),
        P(("role", "head"), "seq"),
        P(("role", "head"), "seq"),
        P(("role", "head"), "seq"),
        P(("role", "head")),
    )
    out_specs = (P(("role", "head"), "seq"), P(("role", "head"), "seq"))
    def chosen(*arrays):
        return fused_body(*arrays) if fits_fused(*arrays) else body(*arrays)

    return jax.shard_map(chosen, mesh=mesh, in_specs=in_specs, out_specs=out_specs, check_vma=False)
```

```python
import functools
import math

import jax
import jax.numpy as jnp
import ml_dtypes
import numpy as np
from jax import lax
from jax.experimental import pallas as pl
from jax.experimental.pallas import tpu as pltpu
from jax.sharding import PartitionSpec as P

WINDOW = 4096
MESH = pl.DeviceIdType.MESH
highest = lax.Precision.HIGHEST


def shifted(value, axis, steps):
    count = lax.axis_size(axis)
    leading, last = (max(0, -steps), min(count, count - steps))
    return lax.ppermute(value, axis, [(source, source + steps) for source in range(leading, last)])


def angle_table(row_ids, col_ids, length):
    product = row_ids[:, None] * col_ids[None, :] % length
    quarter = length // 4
    eighth = length // 8
    quadrant = product // quarter
    within = product % quarter
    flipped = within > eighth
    reduced = jnp.where(flipped, quarter - within, within)
    angles = reduced.astype(jnp.float32) * (2.0 * math.pi / length)
    base_cos = jnp.cos(angles)
    base_sin = jnp.sin(angles)
    first_cos = jnp.where(flipped, base_sin, base_cos)
    first_sin = jnp.where(flipped, base_cos, base_sin)
    cosine = jnp.where(
        quadrant == 0,
        first_cos,
        jnp.where(quadrant == 1, -first_sin, jnp.where(quadrant == 2, -first_cos, first_sin)),
    )
    sine_part = jnp.where(
        quadrant == 0,
        first_sin,
        jnp.where(quadrant == 1, first_cos, jnp.where(quadrant == 2, -first_sin, -first_cos)),
    )
    return (cosine, sine_part)


def spread_rows(stacked):
    pieces = stacked.shape[2]
    cosine, sine_part = angle_table(
        jnp.arange(2 * pieces, dtype=jnp.int32), jnp.arange(pieces, dtype=jnp.int32), 2 * pieces
    )
    real_part = jnp.einsum("kd,ncdr->nckr", cosine, stacked, precision=highest)
    imag_part = -jnp.einsum("kd,ncdr->nckr", sine_part, stacked, precision=highest)
    return (real_part, imag_part)


def twist(real_part, imag_part, freq_ids, time_ids, length, turning):
    cosine, sine_part = angle_table(freq_ids, time_ids, length)
    return (
        real_part * cosine - turning * imag_part * sine_part,
        imag_part * cosine + turning * real_part * sine_part,
    )


def along_block(real_part, imag_part, turning):
    length = real_part.shape[-1]
    cosine, sine_part = angle_table(
        jnp.arange(length, dtype=jnp.int32), jnp.arange(length, dtype=jnp.int32), length
    )
    out_real = jnp.einsum(
        "nckb,bj->nckj", real_part, cosine, precision=highest
    ) - turning * jnp.einsum("nckb,bj->nckj", imag_part, sine_part, precision=highest)
    out_imag = jnp.einsum(
        "nckb,bj->nckj", imag_part, cosine, precision=highest
    ) + turning * jnp.einsum("nckb,bj->nckj", real_part, sine_part, precision=highest)
    return (out_real, out_imag)


def gather_rows(real_part, imag_part, length):
    doubled = real_part.shape[2]
    cosine, sine_part = angle_table(
        jnp.arange(doubled // 2, dtype=jnp.int32), jnp.arange(doubled, dtype=jnp.int32), doubled
    )
    signal = jnp.einsum("dk,nckr->ncdr", cosine, real_part, precision=highest) - jnp.einsum(
        "dk,nckr->ncdr", sine_part, imag_part, precision=highest
    )
    return signal / length


def student(signal, gate_part, taps, target, skip_part, forward, inverse, seq_total):
    spec_real, spec_imag = forward(jnp.stack([signal, taps]))
    input_re, taps_re = (spec_real[0], spec_real[1])
    input_im, taps_im = (spec_imag[0], spec_imag[1])
    conv_re = input_re * taps_re - input_im * taps_im
    conv_im = input_re * taps_im + input_im * taps_re
    convolved = inverse(conv_re[None], conv_im[None])[0]
    output = gate_part * (convolved + skip_part[:, None] * signal)
    backed = gate_part * (output - target)
    back_real, back_imag = forward(backed[None])
    back_re, back_im = (back_real[0], back_imag[0])
    left_re = taps_re * back_re + taps_im * back_im
    left_im = taps_re * back_im - taps_im * back_re
    right_re = input_re * back_re + input_im * back_im
    right_im = input_re * back_im - input_im * back_re
    corrected = inverse(jnp.stack([left_re, right_re]), jnp.stack([left_im, right_im]))
    grad_input = skip_part[:, None] * backed + corrected[0]
    filter_step = corrected[1] * seq_total ** (-0.5)
    return (grad_input, filter_step)


def body(
    query_heads,
    key_heads,
    value_heads,
    distill_proj,
    conv_input,
    gate_input,
    filter_taps,
    skip_gain,
):
    shard_len = query_heads.shape[0]
    kv_local = key_heads.shape[1]
    per_group = query_heads.shape[1] // kv_local
    head_dim = query_heads.shape[2]
    devices = lax.axis_size("seq")
    seq_rank = lax.axis_index("seq")
    shards = min((WINDOW + shard_len - 1) // shard_len, devices - 1)
    per_step = max(1, 512 // shard_len)
    total_shards = -(-(shards + 1) // per_step) * per_step
    own_block = jnp.stack([key_heads, value_heads])
    buffer = jnp.concatenate(
        [jnp.zeros((total_shards - 1,) + own_block.shape, jnp.bfloat16), own_block[None]], axis=0
    )

    def fetch(step_id, carried):
        current, stored = carried
        current = shifted(current, "seq", 1)
        stored = lax.dynamic_update_index_in_dim(stored, current, total_shards - 1 - step_id, 0)
        return (current, stored)

    buffer = lax.fori_loop(1, shards + 1, fetch, (own_block, buffer))[1]
    key_span = per_step * shard_len
    blocks = total_shards // per_step
    keys_all = buffer[:, 0].reshape(blocks, key_span, kv_local, head_dim)
    values_all = buffer[:, 1].reshape(blocks, key_span, kv_local, head_dim)
    first_key = (seq_rank + 1 - total_shards) * shard_len
    query_pos = seq_rank * shard_len + jnp.arange(shard_len, dtype=jnp.int32)
    queries = query_heads.reshape(shard_len, kv_local, per_group, head_dim)
    score_scale = head_dim ** (-0.5)
    block_ids = jnp.arange(blocks, dtype=jnp.int32)

    def online_step(carried, element):
        row_max, row_sum, weighted = carried
        block_id, key_block, value_block = element
        scores = (
            jnp.einsum("qgae,kge->gaqk", queries, key_block, preferred_element_type=jnp.float32)
            * score_scale
        )
        key_pos = first_key + block_id * key_span + jnp.arange(key_span, dtype=jnp.int32)
        in_window = (
            (key_pos[None, :] <= query_pos[:, None])
            & (key_pos[None, :] > query_pos[:, None] - WINDOW)
            & (key_pos[None, :] >= 0)
        )
        new_max = jnp.maximum(row_max, jnp.max(jnp.where(in_window, scores, -jnp.inf), axis=-1))
        safe_max = jnp.where(new_max == -jnp.inf, 0.0, new_max)
        rescale = jnp.exp(row_max - safe_max)
        weight = jnp.where(in_window, jnp.exp(scores - safe_max[..., None]), 0.0)
        row_sum = row_sum * rescale + jnp.sum(weight, axis=-1)
        weighted = weighted * jnp.transpose(rescale, (2, 0, 1))[..., None] + jnp.einsum(
            "gaqk,kge->qgae",
            weight.astype(jnp.bfloat16),
            value_block,
            preferred_element_type=jnp.float32,
        )
        return ((new_max, row_sum, weighted), None)

    start_state = (
        jnp.full((kv_local, per_group, shard_len), -jnp.inf, jnp.float32),
        jnp.zeros((kv_local, per_group, shard_len), jnp.float32),
        jnp.zeros((shard_len, kv_local, per_group, head_dim), jnp.float32),
    )
    final_state = lax.scan(online_step, start_state, (block_ids, keys_all, values_all))[0]
    row_sum, weighted = (final_state[1], final_state[2])
    attended = (
        (weighted / jnp.transpose(row_sum, (2, 0, 1))[..., None])
        .reshape(shard_len, kv_local * per_group, head_dim)
        .astype(jnp.bfloat16)
    )
    target = lax.psum_scatter(
        jnp.einsum("the,hec->ct", attended, distill_proj, preferred_element_type=jnp.float32),
        ("role", "head"),
        scatter_dimension=0,
        tiled=True,
    )
    signal = conv_input.astype(jnp.float32)
    gate_part = gate_input.astype(jnp.float32)
    full_len = 2 * devices * shard_len
    seq_total = devices * shard_len
    freq_all = jnp.arange(2 * devices, dtype=jnp.int32)
    time_all = jnp.arange(shard_len, dtype=jnp.int32)
    part_len = shard_len // devices
    freq_mine = 2 * seq_rank + jnp.arange(2, dtype=jnp.int32)
    time_mine = seq_rank * part_len + jnp.arange(part_len, dtype=jnp.int32)

    def to_rows(stacked):
        return lax.all_to_all(stacked, "seq", split_axis=3, concat_axis=2, tiled=True)

    def to_cols(stacked):
        return lax.all_to_all(stacked, "seq", split_axis=2, concat_axis=3, tiled=True)

    def forward(stacked):
        pieces = stacked.shape[0]
        arrived = to_rows(stacked[:, :, None, :])
        real_part, imag_part = spread_rows(arrived)
        real_part, imag_part = twist(real_part, imag_part, freq_all, time_mine, full_len, -1.0)
        joined = to_cols(jnp.concatenate([real_part, imag_part], axis=0))
        return along_block(joined[:pieces], joined[pieces:], -1.0)

    def inverse(real_part, imag_part):
        pieces = real_part.shape[0]
        real_part, imag_part = along_block(real_part, imag_part, 1.0)
        real_part, imag_part = twist(real_part, imag_part, freq_mine, time_all, full_len, 1.0)
        arrived = to_rows(jnp.concatenate([real_part, imag_part], axis=0))
        rebuilt = gather_rows(arrived[:pieces], arrived[pieces:], full_len)
        return to_cols(rebuilt)[:, :, 0, :]

    grad_input, filter_step = student(
        signal, gate_part, filter_taps, target, skip_gain, forward, inverse, seq_total
    )
    return (grad_input, filter_step)


def half_step_table(length):
    product = np.arange(length)[:, None] * (2 * np.arange(length)[None, :] + 1) % (4 * length)
    angle = product * (math.pi / (2 * length))
    whole = np.concatenate([np.cos(angle), np.sin(angle)], axis=1)
    upper = whole.astype(ml_dtypes.bfloat16)
    lower = (whole - upper.astype(np.float64)).astype(ml_dtypes.bfloat16)
    return np.stack([upper, lower])


def fits_fused(query_heads, key_heads, value_heads, distill_proj, conv_input, gate_input, filter_taps, skip_gain):
    seq_total = lax.axis_size("seq") * query_heads.shape[0]
    groups = lax.axis_size("role") * lax.axis_size("head")
    chan_local = conv_input.shape[0]
    return (
        seq_total <= min(WINDOW, 1024)
        and query_heads.shape[0] % 128 == 0
        and key_heads.shape[1] == 1
        and key_heads.shape[2] % 128 == 0
        and chan_local % 128 == 0
        and chan_local * groups == distill_proj.shape[2]
    )


def dot_nt(left, right):
    return lax.dot_general(left, right, (((1,), (1,)), ((), ())), preferred_element_type=jnp.float32)


def forward(rows, table_buf, where):
    upper = jnp.dot(rows, table_buf[0, where, :], preferred_element_type=jnp.float32)
    return upper + jnp.dot(rows, table_buf[1, where, :], preferred_element_type=jnp.float32)


def inverse(spec, turned_buf):
    upper = spec.astype(jnp.bfloat16)
    lower = (spec - upper.astype(jnp.float32)).astype(jnp.bfloat16)
    width = turned_buf.shape[1] // 2
    wide = jnp.dot(upper, turned_buf[...], preferred_element_type=jnp.float32)
    rest = jnp.dot(lower, turned_buf[:, :width], preferred_element_type=jnp.float32)
    return wide[:, :width] + (wide[:, width:] + rest)


def fused_kernel(
    seq_n, role_n, head_n, heads,
    query_hbm, key_hbm, value_hbm, proj_hbm, signal_hbm, gate_hbm, taps_hbm, skip_hbm, table_hbm, turned_hbm,
    grad_ref, step_ref,
    query_buf, key_buf, value_buf, proj_buf, gate_buf, taps_buf, skip_buf, table_buf, turned_buf,
    pair_buf, spec_buf, out_buf, part_send, part_recv, back_buf,
    local_sem, gather_send, gather_recv, part_send_sem, part_recv_sem, back_send, back_recv,
):
    group_n = role_n * head_n
    mine = lax.axis_index("seq")
    group = lax.axis_index("role") * head_n + lax.axis_index("head")
    span = key_hbm.shape[0]
    chans = gate_buf.shape[0]
    seq_total = seq_n * span
    head_dim = key_hbm.shape[1]
    here = pl.ds(pl.multiple_of(mine * span, span), span)

    def place(rank):
        return pl.ds(pl.multiple_of(rank * span, span), span)

    def seq_peer(step):
        return lax.rem(mine + step, seq_n)

    def seq_from(step):
        return lax.rem(mine + seq_n - step, seq_n)

    def group_peer(step):
        other = lax.rem(group + step, group_n)
        return other, {"role": other // head_n, "head": lax.rem(other, head_n)}

    def group_from(step):
        return lax.rem(group + group_n - step, group_n)

    signal_rows, taps_rows = pl.ds(0, chans), pl.ds(chans, chans)
    locals_ = [
        pltpu.make_async_copy(source, target, local_sem.at[index])
        for index, (source, target) in enumerate([
            (taps_hbm, taps_buf),
            (query_hbm, query_buf),
            (key_hbm, key_buf.at[here]),
            (value_hbm, value_buf.at[here]),
            (signal_hbm, pair_buf.at[signal_rows, here]),
            (proj_hbm, proj_buf),
            (gate_hbm, gate_buf),
            (skip_hbm, skip_buf),
            (table_hbm, table_buf),
            (turned_hbm.at[:, pl.ds(pl.multiple_of(2 * mine * span, 2 * span), 2 * span)], turned_buf),
        ])
    ]
    for copy in locals_:
        copy.start()
    taps_copy, query_copy, key_copy, value_copy, signal_copy, proj_copy, gate_copy, skip_copy, table_copy, turned_copy = locals_

    barrier = pltpu.get_barrier_semaphore()
    for step in range(1, seq_n):
        pl.semaphore_signal(barrier, inc=1, device_id={"seq": seq_peer(step)}, device_id_type=MESH)
    for step in range(1, group_n):
        pl.semaphore_signal(barrier, inc=1, device_id=group_peer(step)[1], device_id_type=MESH)
    taps_copy.wait()
    pair_buf[taps_rows, here] = taps_buf[...].astype(jnp.bfloat16)
    rows = query_buf.shape[0]
    row_id = lax.broadcasted_iota(jnp.int32, (rows, rows), 0)
    col_id = lax.broadcasted_iota(jnp.int32, (rows, rows), 1)
    wanted = (row_id % span) * heads + row_id // span
    order = jnp.where(col_id == wanted, 1.0, 0.0).astype(jnp.bfloat16)
    query_copy.wait()
    queries = jnp.dot(order, query_buf[...], preferred_element_type=jnp.float32).astype(jnp.bfloat16)
    pl.semaphore_wait(barrier, seq_n + group_n - 2)

    gathered = (
        lambda owner: key_buf.at[place(owner)],
        lambda owner: value_buf.at[place(owner)],
        lambda owner: pair_buf.at[signal_rows, place(owner)],
        lambda owner: pair_buf.at[taps_rows, place(owner)],
    )
    sources = (key_hbm, value_hbm, signal_hbm, pair_buf.at[taps_rows, here])

    def gather(kind, step, owner):
        return pltpu.make_async_remote_copy(
            src_ref=sources[kind],
            dst_ref=gathered[kind](owner),
            send_sem=gather_send.at[kind, step],
            recv_sem=gather_recv.at[kind, owner],
            device_id={"seq": seq_peer(step)},
            device_id_type=MESH,
        )

    far_first = sorted(range(1, seq_n), key=lambda step: abs(2 * step - seq_n))
    sends = []

    def send_gather(kind):
        for step in far_first:
            copy = gather(kind, step, mine)
            copy.start()
            sends.append(copy)

    width = 2 if seq_n % 2 == 0 else 1

    def chunk(step):
        first = lax.rem(mine // width + step, seq_n // width) * width
        if step:
            owners = [first + inner for inner in range(width)]
        else:
            owners = [first + lax.rem(mine + 1, 2)] if width == 2 else []
        return first, owners, pl.ds(pl.multiple_of(first * span, width * span), width * span)

    send_gather(0)
    send_gather(1)
    key_copy.wait()
    value_copy.wait()
    for step in range(seq_n // width):
        first, owners, where = chunk(step)
        for owner in owners:
            gather(0, 1, owner).wait_recv()
        scores = dot_nt(queries, key_buf[where, :]) * (head_dim ** -0.5)
        query_pos = mine * span + lax.broadcasted_iota(jnp.int32, scores.shape, 0) % span
        key_pos = first * span + lax.broadcasted_iota(jnp.int32, scores.shape, 1)
        live = key_pos <= query_pos
        scores = jnp.where(live, scores, -jnp.inf)
        chunk_max = jnp.max(scores, axis=1, keepdims=True)
        new_max = jnp.maximum(row_max, chunk_max) if step else chunk_max
        weight = jnp.exp(scores - new_max)
        chunk_sum = jnp.sum(weight, axis=1, keepdims=True)
        for owner in owners:
            gather(1, 1, owner).wait_recv()
        if step == seq_n // width - 1:
            send_gather(2)
            send_gather(3)
        product = jnp.dot(weight.astype(jnp.bfloat16), value_buf[where, :], preferred_element_type=jnp.float32)
        if step:
            rescale = jnp.exp(row_max - new_max)
            row_sum = row_sum * rescale + chunk_sum
            weighted = weighted * rescale + product
        else:
            row_sum, weighted = chunk_sum, product
        row_max = new_max
    attended = (weighted / row_sum).astype(jnp.bfloat16)

    proj_copy.wait()
    def part_copy(other, slot):
        return pltpu.make_async_remote_copy(
            src_ref=part_send.at[other],
            dst_ref=part_recv.at[slot],
            send_sem=part_send_sem.at[other],
            recv_sem=part_recv_sem.at[slot],
            device_id={"role": other // head_n, "head": lax.rem(other, head_n)},
            device_id_type=MESH,
        )

    couple = 2 if group_n % 2 == 0 else 1
    for step in list(range(1, group_n // couple, 2)) + list(range(2, group_n // couple, 2)) + [0]:
        first = lax.rem(group // couple + step, group_n // couple) * couple
        columns = pl.ds(pl.multiple_of(first * chans, couple * chans), couple * chans)
        partial = 0.0
        for head in range(heads):
            partial = partial + jnp.dot(
                attended[head * span:(head + 1) * span],
                proj_buf[head, :, columns],
                preferred_element_type=jnp.float32,
            )
        for inner in range(couple):
            part_send[first + inner] = partial[:, inner * chans:(inner + 1) * chans].astype(jnp.bfloat16)
        if step:
            others = [first + inner for inner in range(couple)]
        else:
            others = [first + lax.rem(group + 1, 2)] if couple == 2 else []
        for other in others:
            copy = part_copy(other, group)
            copy.start()
            sends.append(copy)

    signal_copy.wait()
    for step in range(1, seq_n):
        gather(2, step, seq_from(step)).wait_recv()
        gather(3, step, seq_from(step)).wait_recv()
    table_copy.wait()
    turned_copy.wait()
    gate_copy.wait()
    skip_copy.wait()
    spec_buf[...] = forward(pair_buf[...], table_buf, slice(None))
    low, high = pl.ds(0, seq_total), pl.ds(seq_total, seq_total)
    input_c, input_s = spec_buf[signal_rows, low], spec_buf[signal_rows, high]
    taps_c, taps_s = spec_buf[taps_rows, low], spec_buf[taps_rows, high]
    conv_spec = jnp.concatenate(
        [input_c * taps_c - input_s * taps_s, input_c * taps_s + input_s * taps_c], axis=1
    )
    conv = inverse(conv_spec, turned_buf) * (1.0 / seq_total)
    skip = jnp.transpose(jnp.broadcast_to(skip_buf[...], (span, chans)))
    gate = gate_buf[...].astype(jnp.float32)
    out_buf[...] = gate * (conv + skip * pair_buf[signal_rows, here].astype(jnp.float32))

    target = part_send[group].astype(jnp.float32)
    for step in range(1, group_n):
        source = group_from(step)
        part_copy(source, source).wait_recv()
        target = target + part_recv[source].astype(jnp.float32)
    back = gate * (out_buf[...] - jnp.transpose(target))
    back_buf[:, here] = back.astype(jnp.bfloat16)

    def back_copy(step, owner):
        where = place(owner)
        return pltpu.make_async_remote_copy(
            src_ref=back_buf.at[:, here],
            dst_ref=back_buf.at[:, where],
            send_sem=back_send.at[step],
            recv_sem=back_recv.at[owner],
            device_id={"seq": seq_peer(step)},
            device_id_type=MESH,
        )

    for step in far_first:
        copy = back_copy(step, mine)
        copy.start()
        sends.append(copy)
    back_spec = 0.0
    for step in range(seq_n // width):
        _, owners, where = chunk(step)
        for owner in owners:
            back_copy(1, owner).wait_recv()
        back_spec = back_spec + forward(back_buf[:, where], table_buf, where)
    back_c, back_s = back_spec[:, :seq_total], back_spec[:, seq_total:]

    def correlation(rows):
        first_c, first_s = spec_buf[rows, low], spec_buf[rows, high]
        return jnp.concatenate([first_c * back_c + first_s * back_s, first_c * back_s - first_s * back_c], axis=1)

    lags = inverse(jnp.concatenate([correlation(taps_rows), correlation(signal_rows)], axis=0), turned_buf)
    grad_ref[...] = skip * back + lags[:chans] * (1.0 / seq_total)
    step_ref[...] = lags[chans:] * (seq_total ** -1.5)
    for copy in sends:
        copy.wait_send()


def hand_over(grad_in, step_in, grad_out, step_out, sems):
    copies = [
        pltpu.make_async_copy(grad_in, grad_out, sems.at[0]),
        pltpu.make_async_copy(step_in, step_out, sems.at[1]),
    ]
    for copy in copies:
        copy.start()
    for copy in copies:
        copy.wait()


def fused_body(query_heads, key_heads, value_heads, distill_proj, conv_input, gate_input, filter_taps, skip_gain):
    span, heads, head_dim = query_heads.shape
    seq_n, role_n, head_n = (lax.axis_size(axis) for axis in ("seq", "role", "head"))
    group_n = role_n * head_n
    seq_total = seq_n * span
    chans = conv_input.shape[0]
    table_terms = half_step_table(seq_total)
    table = jnp.asarray(table_terms)
    turned = table_terms.reshape(2, seq_n, span, 2 * seq_total).transpose(3, 1, 0, 2)
    turned = jnp.asarray(np.ascontiguousarray(turned.reshape(2 * seq_total, 2 * seq_total)))
    in_hbm = pl.BlockSpec(memory_space=pltpu.HBM)
    vmem = pl.BlockSpec(memory_space=pltpu.VMEM)
    bf16, f32 = jnp.bfloat16, jnp.float32
    dma = pltpu.SemaphoreType.DMA
    operands = (
        query_heads.reshape(span * heads, head_dim),
        key_heads.reshape(span, head_dim),
        value_heads.reshape(span, head_dim),
        distill_proj,
        conv_input,
        gate_input,
        filter_taps,
        skip_gain.reshape(1, chans),
        table,
        turned,
    )
    results = pl.pallas_call(
        functools.partial(fused_kernel, seq_n, role_n, head_n, heads),
        out_shape=[pltpu.VMEM((chans, span), f32)] * 2,
        in_specs=[in_hbm] * 10,
        out_specs=[vmem, vmem],
        scratch_shapes=[
            pltpu.VMEM((span * heads, head_dim), bf16),
            pltpu.VMEM((seq_total, head_dim), bf16),
            pltpu.VMEM((seq_total, head_dim), bf16),
            pltpu.VMEM(distill_proj.shape, bf16),
            pltpu.VMEM((chans, span), bf16),
            pltpu.VMEM((chans, span), f32),
            pltpu.VMEM((1, chans), f32),
            pltpu.VMEM(table.shape, bf16),
            pltpu.VMEM((2 * seq_total, 2 * span), bf16),
            pltpu.VMEM((2 * chans, seq_total), bf16),
            pltpu.VMEM((2 * chans, 2 * seq_total), f32),
            pltpu.VMEM((chans, span), f32),
            pltpu.VMEM((group_n, span, chans), bf16),
            pltpu.VMEM((group_n, span, chans), bf16),
            pltpu.VMEM((chans, seq_total), bf16),
            dma((10,)),
            dma((4, seq_n)),
            dma((4, seq_n)),
            dma((group_n,)),
            dma((group_n,)),
            dma((seq_n,)),
            dma((seq_n,)),
        ],
        compiler_params=pltpu.CompilerParams(
            collective_id=0, has_side_effects=True, vmem_limit_bytes=40 * 1024 * 1024
        ),
    )(*[pltpu.with_memory_space_constraint(operand, pltpu.HBM) for operand in operands])
    return pl.pallas_call(
        hand_over,
        out_shape=[jax.ShapeDtypeStruct((chans, span), f32)] * 2,
        in_specs=[pl.BlockSpec(memory_space=pl.ANY)] * 2,
        out_specs=[in_hbm] * 2,
        scratch_shapes=[dma((2,))],
        compiler_params=pltpu.CompilerParams(vmem_limit_bytes=40 * 1024 * 1024),
    )(*results)


def solution(mesh):
    in_specs = (
        P("seq", ("role", "head"), None),
        P("seq", ("role", "head"), None),
        P("seq", ("role", "head"), None),
        P(("role", "head"), None, None),
        P(("role", "head"), "seq"),
        P(("role", "head"), "seq"),
        P(("role", "head"), "seq"),
        P(("role", "head")),
    )
    out_specs = (P(("role", "head"), "seq"), P(("role", "head"), "seq"))
    def chosen(*arrays):
        return fused_body(*arrays) if fits_fused(*arrays) else body(*arrays)

    return jax.shard_map(chosen, mesh=mesh, in_specs=in_specs, out_specs=out_specs, check_vma=False)
```

```python
import functools
import math

import jax
import jax.numpy as jnp
import ml_dtypes
import numpy as np
from jax import lax
from jax.experimental import pallas as pl
from jax.experimental.pallas import tpu as pltpu
from jax.sharding import PartitionSpec as P

WINDOW = 4096
MESH = pl.DeviceIdType.MESH
highest = lax.Precision.HIGHEST


def shifted(value, axis, steps):
    count = lax.axis_size(axis)
    leading, last = (max(0, -steps), min(count, count - steps))
    return lax.ppermute(value, axis, [(source, source + steps) for source in range(leading, last)])


def angle_table(row_ids, col_ids, length):
    product = row_ids[:, None] * col_ids[None, :] % length
    quarter = length // 4
    eighth = length // 8
    quadrant = product // quarter
    within = product % quarter
    flipped = within > eighth
    reduced = jnp.where(flipped, quarter - within, within)
    angles = reduced.astype(jnp.float32) * (2.0 * math.pi / length)
    base_cos = jnp.cos(angles)
    base_sin = jnp.sin(angles)
    first_cos = jnp.where(flipped, base_sin, base_cos)
    first_sin = jnp.where(flipped, base_cos, base_sin)
    cosine = jnp.where(
        quadrant == 0,
        first_cos,
        jnp.where(quadrant == 1, -first_sin, jnp.where(quadrant == 2, -first_cos, first_sin)),
    )
    sine_part = jnp.where(
        quadrant == 0,
        first_sin,
        jnp.where(quadrant == 1, first_cos, jnp.where(quadrant == 2, -first_sin, -first_cos)),
    )
    return (cosine, sine_part)


def spread_rows(stacked):
    pieces = stacked.shape[2]
    cosine, sine_part = angle_table(
        jnp.arange(2 * pieces, dtype=jnp.int32), jnp.arange(pieces, dtype=jnp.int32), 2 * pieces
    )
    real_part = jnp.einsum("kd,ncdr->nckr", cosine, stacked, precision=highest)
    imag_part = -jnp.einsum("kd,ncdr->nckr", sine_part, stacked, precision=highest)
    return (real_part, imag_part)


def twist(real_part, imag_part, freq_ids, time_ids, length, turning):
    cosine, sine_part = angle_table(freq_ids, time_ids, length)
    return (
        real_part * cosine - turning * imag_part * sine_part,
        imag_part * cosine + turning * real_part * sine_part,
    )


def along_block(real_part, imag_part, turning):
    length = real_part.shape[-1]
    cosine, sine_part = angle_table(
        jnp.arange(length, dtype=jnp.int32), jnp.arange(length, dtype=jnp.int32), length
    )
    out_real = jnp.einsum(
        "nckb,bj->nckj", real_part, cosine, precision=highest
    ) - turning * jnp.einsum("nckb,bj->nckj", imag_part, sine_part, precision=highest)
    out_imag = jnp.einsum(
        "nckb,bj->nckj", imag_part, cosine, precision=highest
    ) + turning * jnp.einsum("nckb,bj->nckj", real_part, sine_part, precision=highest)
    return (out_real, out_imag)


def gather_rows(real_part, imag_part, length):
    doubled = real_part.shape[2]
    cosine, sine_part = angle_table(
        jnp.arange(doubled // 2, dtype=jnp.int32), jnp.arange(doubled, dtype=jnp.int32), doubled
    )
    signal = jnp.einsum("dk,nckr->ncdr", cosine, real_part, precision=highest) - jnp.einsum(
        "dk,nckr->ncdr", sine_part, imag_part, precision=highest
    )
    return signal / length


def student(signal, gate_part, taps, target, skip_part, forward, inverse, seq_total):
    spec_real, spec_imag = forward(jnp.stack([signal, taps]))
    input_re, taps_re = (spec_real[0], spec_real[1])
    input_im, taps_im = (spec_imag[0], spec_imag[1])
    conv_re = input_re * taps_re - input_im * taps_im
    conv_im = input_re * taps_im + input_im * taps_re
    convolved = inverse(conv_re[None], conv_im[None])[0]
    output = gate_part * (convolved + skip_part[:, None] * signal)
    backed = gate_part * (output - target)
    back_real, back_imag = forward(backed[None])
    back_re, back_im = (back_real[0], back_imag[0])
    left_re = taps_re * back_re + taps_im * back_im
    left_im = taps_re * back_im - taps_im * back_re
    right_re = input_re * back_re + input_im * back_im
    right_im = input_re * back_im - input_im * back_re
    corrected = inverse(jnp.stack([left_re, right_re]), jnp.stack([left_im, right_im]))
    grad_input = skip_part[:, None] * backed + corrected[0]
    filter_step = corrected[1] * seq_total ** (-0.5)
    return (grad_input, filter_step)


def body(
    query_heads,
    key_heads,
    value_heads,
    distill_proj,
    conv_input,
    gate_input,
    filter_taps,
    skip_gain,
):
    shard_len = query_heads.shape[0]
    kv_local = key_heads.shape[1]
    per_group = query_heads.shape[1] // kv_local
    head_dim = query_heads.shape[2]
    devices = lax.axis_size("seq")
    seq_rank = lax.axis_index("seq")
    shards = min((WINDOW + shard_len - 1) // shard_len, devices - 1)
    per_step = max(1, 512 // shard_len)
    total_shards = -(-(shards + 1) // per_step) * per_step
    own_block = jnp.stack([key_heads, value_heads])
    buffer = jnp.concatenate(
        [jnp.zeros((total_shards - 1,) + own_block.shape, jnp.bfloat16), own_block[None]], axis=0
    )

    def fetch(step_id, carried):
        current, stored = carried
        current = shifted(current, "seq", 1)
        stored = lax.dynamic_update_index_in_dim(stored, current, total_shards - 1 - step_id, 0)
        return (current, stored)

    buffer = lax.fori_loop(1, shards + 1, fetch, (own_block, buffer))[1]
    key_span = per_step * shard_len
    blocks = total_shards // per_step
    keys_all = buffer[:, 0].reshape(blocks, key_span, kv_local, head_dim)
    values_all = buffer[:, 1].reshape(blocks, key_span, kv_local, head_dim)
    first_key = (seq_rank + 1 - total_shards) * shard_len
    query_pos = seq_rank * shard_len + jnp.arange(shard_len, dtype=jnp.int32)
    queries = query_heads.reshape(shard_len, kv_local, per_group, head_dim)
    score_scale = head_dim ** (-0.5)
    block_ids = jnp.arange(blocks, dtype=jnp.int32)

    def online_step(carried, element):
        row_max, row_sum, weighted = carried
        block_id, key_block, value_block = element
        scores = (
            jnp.einsum("qgae,kge->gaqk", queries, key_block, preferred_element_type=jnp.float32)
            * score_scale
        )
        key_pos = first_key + block_id * key_span + jnp.arange(key_span, dtype=jnp.int32)
        in_window = (
            (key_pos[None, :] <= query_pos[:, None])
            & (key_pos[None, :] > query_pos[:, None] - WINDOW)
            & (key_pos[None, :] >= 0)
        )
        new_max = jnp.maximum(row_max, jnp.max(jnp.where(in_window, scores, -jnp.inf), axis=-1))
        safe_max = jnp.where(new_max == -jnp.inf, 0.0, new_max)
        rescale = jnp.exp(row_max - safe_max)
        weight = jnp.where(in_window, jnp.exp(scores - safe_max[..., None]), 0.0)
        row_sum = row_sum * rescale + jnp.sum(weight, axis=-1)
        weighted = weighted * jnp.transpose(rescale, (2, 0, 1))[..., None] + jnp.einsum(
            "gaqk,kge->qgae",
            weight.astype(jnp.bfloat16),
            value_block,
            preferred_element_type=jnp.float32,
        )
        return ((new_max, row_sum, weighted), None)

    start_state = (
        jnp.full((kv_local, per_group, shard_len), -jnp.inf, jnp.float32),
        jnp.zeros((kv_local, per_group, shard_len), jnp.float32),
        jnp.zeros((shard_len, kv_local, per_group, head_dim), jnp.float32),
    )
    final_state = lax.scan(online_step, start_state, (block_ids, keys_all, values_all))[0]
    row_sum, weighted = (final_state[1], final_state[2])
    attended = (
        (weighted / jnp.transpose(row_sum, (2, 0, 1))[..., None])
        .reshape(shard_len, kv_local * per_group, head_dim)
        .astype(jnp.bfloat16)
    )
    target = lax.psum_scatter(
        jnp.einsum("the,hec->ct", attended, distill_proj, preferred_element_type=jnp.float32),
        ("role", "head"),
        scatter_dimension=0,
        tiled=True,
    )
    signal = conv_input.astype(jnp.float32)
    gate_part = gate_input.astype(jnp.float32)
    full_len = 2 * devices * shard_len
    seq_total = devices * shard_len
    freq_all = jnp.arange(2 * devices, dtype=jnp.int32)
    time_all = jnp.arange(shard_len, dtype=jnp.int32)
    part_len = shard_len // devices
    freq_mine = 2 * seq_rank + jnp.arange(2, dtype=jnp.int32)
    time_mine = seq_rank * part_len + jnp.arange(part_len, dtype=jnp.int32)

    def to_rows(stacked):
        return lax.all_to_all(stacked, "seq", split_axis=3, concat_axis=2, tiled=True)

    def to_cols(stacked):
        return lax.all_to_all(stacked, "seq", split_axis=2, concat_axis=3, tiled=True)

    def forward(stacked):
        pieces = stacked.shape[0]
        arrived = to_rows(stacked[:, :, None, :])
        real_part, imag_part = spread_rows(arrived)
        real_part, imag_part = twist(real_part, imag_part, freq_all, time_mine, full_len, -1.0)
        joined = to_cols(jnp.concatenate([real_part, imag_part], axis=0))
        return along_block(joined[:pieces], joined[pieces:], -1.0)

    def inverse(real_part, imag_part):
        pieces = real_part.shape[0]
        real_part, imag_part = along_block(real_part, imag_part, 1.0)
        real_part, imag_part = twist(real_part, imag_part, freq_mine, time_all, full_len, 1.0)
        arrived = to_rows(jnp.concatenate([real_part, imag_part], axis=0))
        rebuilt = gather_rows(arrived[:pieces], arrived[pieces:], full_len)
        return to_cols(rebuilt)[:, :, 0, :]

    grad_input, filter_step = student(
        signal, gate_part, filter_taps, target, skip_gain, forward, inverse, seq_total
    )
    return (grad_input, filter_step)


def half_step_table(length):
    product = np.arange(length)[:, None] * (2 * np.arange(length)[None, :] + 1) % (4 * length)
    angle = product * (math.pi / (2 * length))
    whole = np.concatenate([np.cos(angle), np.sin(angle)], axis=1)
    upper = whole.astype(ml_dtypes.bfloat16)
    lower = (whole - upper.astype(np.float64)).astype(ml_dtypes.bfloat16)
    return np.stack([upper, lower])


def fits_fused(query_heads, key_heads, value_heads, distill_proj, conv_input, gate_input, filter_taps, skip_gain):
    seq_total = lax.axis_size("seq") * query_heads.shape[0]
    groups = lax.axis_size("role") * lax.axis_size("head")
    chan_local = conv_input.shape[0]
    return (
        seq_total <= min(WINDOW, 1024)
        and query_heads.shape[0] % 128 == 0
        and key_heads.shape[1] == 1
        and key_heads.shape[2] % 128 == 0
        and chan_local % 128 == 0
        and chan_local * groups == distill_proj.shape[2]
    )


def dot_nt(left, right):
    return lax.dot_general(left, right, (((1,), (1,)), ((), ())), preferred_element_type=jnp.float32)


def forward(rows, table_buf, where):
    upper = jnp.dot(rows, table_buf[0, where, :], preferred_element_type=jnp.float32)
    return upper + jnp.dot(rows, table_buf[1, where, :], preferred_element_type=jnp.float32)


def inverse(spec, turned_buf):
    upper = spec.astype(jnp.bfloat16)
    lower = (spec - upper.astype(jnp.float32)).astype(jnp.bfloat16)
    width = turned_buf.shape[1] // 2
    wide = jnp.dot(upper, turned_buf[...], preferred_element_type=jnp.float32)
    rest = jnp.dot(lower, turned_buf[:, :width], preferred_element_type=jnp.float32)
    return wide[:, :width] + (wide[:, width:] + rest)


def fused_kernel(
    seq_n, role_n, head_n, heads,
    query_hbm, key_hbm, value_hbm, proj_hbm, signal_hbm, gate_hbm, taps_hbm, skip_hbm, table_hbm, turned_hbm,
    grad_ref, step_ref,
    query_buf, key_buf, value_buf, proj_buf, gate_buf, taps_buf, skip_buf, table_buf, turned_buf,
    pair_buf, spec_buf, out_buf, part_send, part_recv, back_buf,
    local_sem, gather_send, gather_recv, part_send_sem, part_recv_sem, back_send, back_recv,
):
    group_n = role_n * head_n
    mine = lax.axis_index("seq")
    group = lax.axis_index("role") * head_n + lax.axis_index("head")
    span = key_hbm.shape[0]
    chans = gate_buf.shape[0]
    seq_total = seq_n * span
    head_dim = key_hbm.shape[1]
    here = pl.ds(pl.multiple_of(mine * span, span), span)

    def place(rank):
        return pl.ds(pl.multiple_of(rank * span, span), span)

    def seq_peer(step):
        return lax.rem(mine + step, seq_n)

    def seq_from(step):
        return lax.rem(mine + seq_n - step, seq_n)

    def group_peer(step):
        other = lax.rem(group + step, group_n)
        return other, {"role": other // head_n, "head": lax.rem(other, head_n)}

    def group_from(step):
        return lax.rem(group + group_n - step, group_n)

    signal_rows, taps_rows = pl.ds(0, chans), pl.ds(chans, chans)
    locals_ = [
        pltpu.make_async_copy(source, target, local_sem.at[index])
        for index, (source, target) in enumerate([
            (taps_hbm, taps_buf),
            (query_hbm, query_buf),
            (key_hbm, key_buf.at[here]),
            (value_hbm, value_buf.at[here]),
            (signal_hbm, pair_buf.at[signal_rows, here]),
            (proj_hbm, proj_buf),
            (gate_hbm, gate_buf),
            (skip_hbm, skip_buf),
            (table_hbm, table_buf),
            (turned_hbm.at[:, pl.ds(pl.multiple_of(2 * mine * span, 2 * span), 2 * span)], turned_buf),
        ])
    ]
    for copy in locals_:
        copy.start()
    taps_copy, query_copy, key_copy, value_copy, signal_copy, proj_copy, gate_copy, skip_copy, table_copy, turned_copy = locals_

    barrier = pltpu.get_barrier_semaphore()
    for step in range(1, seq_n):
        pl.semaphore_signal(barrier, inc=1, device_id={"seq": seq_peer(step)}, device_id_type=MESH)
    for step in range(1, group_n):
        pl.semaphore_signal(barrier, inc=1, device_id=group_peer(step)[1], device_id_type=MESH)
    taps_copy.wait()
    pair_buf[taps_rows, here] = taps_buf[...].astype(jnp.bfloat16)
    half_span = span // 2
    part_rows = heads * half_span
    rows = query_buf.shape[0]
    row_id = lax.broadcasted_iota(jnp.int32, (rows, rows), 0)
    col_id = lax.broadcasted_iota(jnp.int32, (rows, rows), 1)
    wanted = (row_id // part_rows * half_span + row_id % half_span) * heads + row_id % part_rows // half_span
    order = jnp.where(col_id == wanted, 1.0, 0.0).astype(jnp.bfloat16)
    query_copy.wait()
    queries = jnp.dot(order, query_buf[...], preferred_element_type=jnp.float32).astype(jnp.bfloat16)
    pl.semaphore_wait(barrier, seq_n + group_n - 2)

    gathered = (
        lambda owner: key_buf.at[place(owner)],
        lambda owner: value_buf.at[place(owner)],
        lambda owner: pair_buf.at[signal_rows, place(owner)],
        lambda owner: pair_buf.at[taps_rows, place(owner)],
    )
    sources = (key_hbm, value_hbm, signal_hbm, pair_buf.at[taps_rows, here])

    def gather(kind, step, owner):
        return pltpu.make_async_remote_copy(
            src_ref=sources[kind],
            dst_ref=gathered[kind](owner),
            send_sem=gather_send.at[kind, step],
            recv_sem=gather_recv.at[kind, owner],
            device_id={"seq": seq_peer(step)},
            device_id_type=MESH,
        )

    far_first = sorted(range(1, seq_n), key=lambda step: abs(2 * step - seq_n))
    sends = []

    def send_gather(kind):
        for step in far_first:
            copy = gather(kind, step, mine)
            copy.start()
            sends.append(copy)

    width = 2 if seq_n % 2 == 0 else 1

    def chunk(step):
        first = lax.rem(mine // width + step, seq_n // width) * width
        if step:
            owners = [first + inner for inner in range(width)]
        else:
            owners = [first + lax.rem(mine + 1, 2)] if width == 2 else []
        return first, owners, pl.ds(pl.multiple_of(first * span, width * span), width * span)

    send_gather(0)
    send_gather(1)
    key_copy.wait()
    value_copy.wait()
    chunks = seq_n // width

    def attend(step, begin, end, state):
        first, _, where = chunk(step)
        scores = dot_nt(queries[begin:end], key_buf[where, :]) * (head_dim ** -0.5)
        row = begin + lax.broadcasted_iota(jnp.int32, scores.shape, 0)
        query_pos = mine * span + row // part_rows * half_span + row % half_span
        key_pos = first * span + lax.broadcasted_iota(jnp.int32, scores.shape, 1)
        scores = jnp.where(key_pos <= query_pos, scores, -jnp.inf)
        new_max = jnp.max(scores, axis=1, keepdims=True)
        if state is not None:
            new_max = jnp.maximum(new_max, state[0][begin:end])
        weight = jnp.exp(scores - new_max)
        row_sum = jnp.sum(weight, axis=1, keepdims=True)
        weighted = jnp.dot(weight.astype(jnp.bfloat16), value_buf[where, :], preferred_element_type=jnp.float32)
        if state is not None:
            rescale = jnp.exp(state[0][begin:end] - new_max)
            row_sum = row_sum + state[1][begin:end] * rescale
            weighted = weighted + state[2][begin:end] * rescale
        return new_max, row_sum, weighted

    state = None
    for step in range(chunks):
        for owner in chunk(step)[1]:
            gather(0, 1, owner).wait_recv()
            gather(1, 1, owner).wait_recv()
        if step < chunks - 1:
            state = attend(step, 0, rows, state)
    send_gather(2)
    send_gather(3)
    proj_copy.wait()

    def part_copy(other, slot, half):
        piece = pl.ds(half * half_span, half_span)
        return pltpu.make_async_remote_copy(
            src_ref=part_send.at[other, piece],
            dst_ref=part_recv.at[slot, piece],
            send_sem=part_send_sem.at[other, half],
            recv_sem=part_recv_sem.at[slot, half],
            device_id={"role": other // head_n, "head": lax.rem(other, head_n)},
            device_id_type=MESH,
        )

    couple = 2 if group_n % 2 == 0 else 1
    couples = group_n // couple
    for half in range(2):
        begin = half * part_rows
        _, row_sum, weighted = attend(chunks - 1, begin, begin + part_rows, state)
        attended = (weighted / row_sum).astype(jnp.bfloat16)
        attended = jnp.concatenate(
            [attended[head * half_span:(head + 1) * half_span] for head in range(heads)], axis=1
        )
        for step in list(range(1, couples, 2)) + list(range(2, couples, 2)) + [0]:
            first = lax.rem(group // couple + step, couples) * couple
            columns = pl.ds(pl.multiple_of(first * chans, couple * chans), couple * chans)
            partial = jnp.dot(attended, proj_buf[:, columns], preferred_element_type=jnp.float32)
            for inner in range(couple):
                part_send[first + inner, pl.ds(half * half_span, half_span)] = partial[
                    :, inner * chans:(inner + 1) * chans
                ].astype(jnp.bfloat16)
            if step:
                others = [first + inner for inner in range(couple)]
            else:
                others = [first + lax.rem(group + 1, 2)] if couple == 2 else []
            for other in others:
                copy = part_copy(other, group, half)
                copy.start()
                sends.append(copy)

    signal_copy.wait()
    for step in range(1, seq_n):
        gather(2, step, seq_from(step)).wait_recv()
        gather(3, step, seq_from(step)).wait_recv()
    table_copy.wait()
    turned_copy.wait()
    gate_copy.wait()
    skip_copy.wait()
    spec_buf[...] = forward(pair_buf[...], table_buf, slice(None))
    low, high = pl.ds(0, seq_total), pl.ds(seq_total, seq_total)
    input_c, input_s = spec_buf[signal_rows, low], spec_buf[signal_rows, high]
    taps_c, taps_s = spec_buf[taps_rows, low], spec_buf[taps_rows, high]
    conv_spec = jnp.concatenate(
        [input_c * taps_c - input_s * taps_s, input_c * taps_s + input_s * taps_c], axis=1
    )
    conv = inverse(conv_spec, turned_buf) * (1.0 / seq_total)
    skip = jnp.transpose(jnp.broadcast_to(skip_buf[...], (span, chans)))
    gate = gate_buf[...].astype(jnp.float32)
    out_buf[...] = gate * (conv + skip * pair_buf[signal_rows, here].astype(jnp.float32))

    target = part_send[group].astype(jnp.float32)
    for step in range(1, group_n):
        source = group_from(step)
        part_copy(source, source, 0).wait_recv()
        part_copy(source, source, 1).wait_recv()
        target = target + part_recv[source].astype(jnp.float32)
    back = gate * (out_buf[...] - jnp.transpose(target))
    back_buf[:, here] = back.astype(jnp.bfloat16)

    def back_copy(step, owner):
        where = place(owner)
        return pltpu.make_async_remote_copy(
            src_ref=back_buf.at[:, here],
            dst_ref=back_buf.at[:, where],
            send_sem=back_send.at[step],
            recv_sem=back_recv.at[owner],
            device_id={"seq": seq_peer(step)},
            device_id_type=MESH,
        )

    for step in far_first:
        copy = back_copy(step, mine)
        copy.start()
        sends.append(copy)
    back_spec = 0.0
    for step in range(seq_n // width):
        _, owners, where = chunk(step)
        for owner in owners:
            back_copy(1, owner).wait_recv()
        back_spec = back_spec + forward(back_buf[:, where], table_buf, where)
    back_c, back_s = back_spec[:, :seq_total], back_spec[:, seq_total:]

    def correlation(rows):
        first_c, first_s = spec_buf[rows, low], spec_buf[rows, high]
        return jnp.concatenate([first_c * back_c + first_s * back_s, first_c * back_s - first_s * back_c], axis=1)

    lags = inverse(jnp.concatenate([correlation(taps_rows), correlation(signal_rows)], axis=0), turned_buf)
    grad_ref[...] = skip * back + lags[:chans] * (1.0 / seq_total)
    step_ref[...] = lags[chans:] * (seq_total ** -1.5)
    for copy in sends:
        copy.wait_send()


def hand_over(grad_in, step_in, grad_out, step_out, sems):
    copies = [
        pltpu.make_async_copy(grad_in, grad_out, sems.at[0]),
        pltpu.make_async_copy(step_in, step_out, sems.at[1]),
    ]
    for copy in copies:
        copy.start()
    for copy in copies:
        copy.wait()


def fused_body(query_heads, key_heads, value_heads, distill_proj, conv_input, gate_input, filter_taps, skip_gain):
    span, heads, head_dim = query_heads.shape
    seq_n, role_n, head_n = (lax.axis_size(axis) for axis in ("seq", "role", "head"))
    group_n = role_n * head_n
    seq_total = seq_n * span
    chans = conv_input.shape[0]
    table_terms = half_step_table(seq_total)
    table = jnp.asarray(table_terms)
    turned = table_terms.reshape(2, seq_n, span, 2 * seq_total).transpose(3, 1, 0, 2)
    turned = jnp.asarray(np.ascontiguousarray(turned.reshape(2 * seq_total, 2 * seq_total)))
    in_hbm = pl.BlockSpec(memory_space=pltpu.HBM)
    vmem = pl.BlockSpec(memory_space=pltpu.VMEM)
    bf16, f32 = jnp.bfloat16, jnp.float32
    dma = pltpu.SemaphoreType.DMA
    operands = (
        query_heads.reshape(span * heads, head_dim),
        key_heads.reshape(span, head_dim),
        value_heads.reshape(span, head_dim),
        distill_proj.reshape(heads * head_dim, distill_proj.shape[2]),
        conv_input,
        gate_input,
        filter_taps,
        skip_gain.reshape(1, chans),
        table,
        turned,
    )
    results = pl.pallas_call(
        functools.partial(fused_kernel, seq_n, role_n, head_n, heads),
        out_shape=[pltpu.VMEM((chans, span), f32)] * 2,
        in_specs=[in_hbm] * 10,
        out_specs=[vmem, vmem],
        scratch_shapes=[
            pltpu.VMEM((span * heads, head_dim), bf16),
            pltpu.VMEM((seq_total, head_dim), bf16),
            pltpu.VMEM((seq_total, head_dim), bf16),
            pltpu.VMEM((heads * head_dim, distill_proj.shape[2]), bf16),
            pltpu.VMEM((chans, span), bf16),
            pltpu.VMEM((chans, span), f32),
            pltpu.VMEM((1, chans), f32),
            pltpu.VMEM(table.shape, bf16),
            pltpu.VMEM((2 * seq_total, 2 * span), bf16),
            pltpu.VMEM((2 * chans, seq_total), bf16),
            pltpu.VMEM((2 * chans, 2 * seq_total), f32),
            pltpu.VMEM((chans, span), f32),
            pltpu.VMEM((group_n, span, chans), bf16),
            pltpu.VMEM((group_n, span, chans), bf16),
            pltpu.VMEM((chans, seq_total), bf16),
            dma((10,)),
            dma((4, seq_n)),
            dma((4, seq_n)),
            dma((group_n, 2)),
            dma((group_n, 2)),
            dma((seq_n,)),
            dma((seq_n,)),
        ],
        compiler_params=pltpu.CompilerParams(
            collective_id=0, has_side_effects=True, vmem_limit_bytes=40 * 1024 * 1024
        ),
    )(*[pltpu.with_memory_space_constraint(operand, pltpu.HBM) for operand in operands])
    return pl.pallas_call(
        hand_over,
        out_shape=[jax.ShapeDtypeStruct((chans, span), f32)] * 2,
        in_specs=[pl.BlockSpec(memory_space=pl.ANY)] * 2,
        out_specs=[in_hbm] * 2,
        scratch_shapes=[dma((2,))],
        compiler_params=pltpu.CompilerParams(vmem_limit_bytes=40 * 1024 * 1024),
    )(*results)


def solution(mesh):
    in_specs = (
        P("seq", ("role", "head"), None),
        P("seq", ("role", "head"), None),
        P("seq", ("role", "head"), None),
        P(("role", "head"), None, None),
        P(("role", "head"), "seq"),
        P(("role", "head"), "seq"),
        P(("role", "head"), "seq"),
        P(("role", "head")),
    )
    out_specs = (P(("role", "head"), "seq"), P(("role", "head"), "seq"))
    def chosen(*arrays):
        return fused_body(*arrays) if fits_fused(*arrays) else body(*arrays)

    return jax.shard_map(chosen, mesh=mesh, in_specs=in_specs, out_specs=out_specs, check_vma=False)
```

```python
import functools
import math

import jax
import jax.numpy as jnp
import ml_dtypes
import numpy as np
from jax import lax
from jax.experimental import pallas as pl
from jax.experimental.pallas import tpu as pltpu
from jax.sharding import PartitionSpec as P

WINDOW = 4096
MESH = pl.DeviceIdType.MESH
highest = lax.Precision.HIGHEST


def shifted(value, axis, steps):
    count = lax.axis_size(axis)
    leading, last = (max(0, -steps), min(count, count - steps))
    return lax.ppermute(value, axis, [(source, source + steps) for source in range(leading, last)])


def angle_table(row_ids, col_ids, length):
    product = row_ids[:, None] * col_ids[None, :] % length
    quarter = length // 4
    eighth = length // 8
    quadrant = product // quarter
    within = product % quarter
    flipped = within > eighth
    reduced = jnp.where(flipped, quarter - within, within)
    angles = reduced.astype(jnp.float32) * (2.0 * math.pi / length)
    base_cos = jnp.cos(angles)
    base_sin = jnp.sin(angles)
    first_cos = jnp.where(flipped, base_sin, base_cos)
    first_sin = jnp.where(flipped, base_cos, base_sin)
    cosine = jnp.where(
        quadrant == 0,
        first_cos,
        jnp.where(quadrant == 1, -first_sin, jnp.where(quadrant == 2, -first_cos, first_sin)),
    )
    sine_part = jnp.where(
        quadrant == 0,
        first_sin,
        jnp.where(quadrant == 1, first_cos, jnp.where(quadrant == 2, -first_sin, -first_cos)),
    )
    return (cosine, sine_part)


def spread_rows(stacked):
    pieces = stacked.shape[2]
    cosine, sine_part = angle_table(
        jnp.arange(2 * pieces, dtype=jnp.int32), jnp.arange(pieces, dtype=jnp.int32), 2 * pieces
    )
    real_part = jnp.einsum("kd,ncdr->nckr", cosine, stacked, precision=highest)
    imag_part = -jnp.einsum("kd,ncdr->nckr", sine_part, stacked, precision=highest)
    return (real_part, imag_part)


def twist(real_part, imag_part, freq_ids, time_ids, length, turning):
    cosine, sine_part = angle_table(freq_ids, time_ids, length)
    return (
        real_part * cosine - turning * imag_part * sine_part,
        imag_part * cosine + turning * real_part * sine_part,
    )


def along_block(real_part, imag_part, turning):
    length = real_part.shape[-1]
    cosine, sine_part = angle_table(
        jnp.arange(length, dtype=jnp.int32), jnp.arange(length, dtype=jnp.int32), length
    )
    out_real = jnp.einsum(
        "nckb,bj->nckj", real_part, cosine, precision=highest
    ) - turning * jnp.einsum("nckb,bj->nckj", imag_part, sine_part, precision=highest)
    out_imag = jnp.einsum(
        "nckb,bj->nckj", imag_part, cosine, precision=highest
    ) + turning * jnp.einsum("nckb,bj->nckj", real_part, sine_part, precision=highest)
    return (out_real, out_imag)


def gather_rows(real_part, imag_part, length):
    doubled = real_part.shape[2]
    cosine, sine_part = angle_table(
        jnp.arange(doubled // 2, dtype=jnp.int32), jnp.arange(doubled, dtype=jnp.int32), doubled
    )
    signal = jnp.einsum("dk,nckr->ncdr", cosine, real_part, precision=highest) - jnp.einsum(
        "dk,nckr->ncdr", sine_part, imag_part, precision=highest
    )
    return signal / length


def student(signal, gate_part, taps, target, skip_part, forward, inverse, seq_total):
    spec_real, spec_imag = forward(jnp.stack([signal, taps]))
    input_re, taps_re = (spec_real[0], spec_real[1])
    input_im, taps_im = (spec_imag[0], spec_imag[1])
    conv_re = input_re * taps_re - input_im * taps_im
    conv_im = input_re * taps_im + input_im * taps_re
    convolved = inverse(conv_re[None], conv_im[None])[0]
    output = gate_part * (convolved + skip_part[:, None] * signal)
    backed = gate_part * (output - target)
    back_real, back_imag = forward(backed[None])
    back_re, back_im = (back_real[0], back_imag[0])
    left_re = taps_re * back_re + taps_im * back_im
    left_im = taps_re * back_im - taps_im * back_re
    right_re = input_re * back_re + input_im * back_im
    right_im = input_re * back_im - input_im * back_re
    corrected = inverse(jnp.stack([left_re, right_re]), jnp.stack([left_im, right_im]))
    grad_input = skip_part[:, None] * backed + corrected[0]
    filter_step = corrected[1] * seq_total ** (-0.5)
    return (grad_input, filter_step)


def body(
    query_heads,
    key_heads,
    value_heads,
    distill_proj,
    conv_input,
    gate_input,
    filter_taps,
    skip_gain,
):
    shard_len = query_heads.shape[0]
    kv_local = key_heads.shape[1]
    per_group = query_heads.shape[1] // kv_local
    head_dim = query_heads.shape[2]
    devices = lax.axis_size("seq")
    seq_rank = lax.axis_index("seq")
    shards = min((WINDOW + shard_len - 1) // shard_len, devices - 1)
    per_step = max(1, 512 // shard_len)
    total_shards = -(-(shards + 1) // per_step) * per_step
    own_block = jnp.stack([key_heads, value_heads])
    buffer = jnp.concatenate(
        [jnp.zeros((total_shards - 1,) + own_block.shape, jnp.bfloat16), own_block[None]], axis=0
    )

    def fetch(step_id, carried):
        current, stored = carried
        current = shifted(current, "seq", 1)
        stored = lax.dynamic_update_index_in_dim(stored, current, total_shards - 1 - step_id, 0)
        return (current, stored)

    buffer = lax.fori_loop(1, shards + 1, fetch, (own_block, buffer))[1]
    key_span = per_step * shard_len
    blocks = total_shards // per_step
    keys_all = buffer[:, 0].reshape(blocks, key_span, kv_local, head_dim)
    values_all = buffer[:, 1].reshape(blocks, key_span, kv_local, head_dim)
    first_key = (seq_rank + 1 - total_shards) * shard_len
    query_pos = seq_rank * shard_len + jnp.arange(shard_len, dtype=jnp.int32)
    queries = query_heads.reshape(shard_len, kv_local, per_group, head_dim)
    score_scale = head_dim ** (-0.5)
    block_ids = jnp.arange(blocks, dtype=jnp.int32)

    def online_step(carried, element):
        row_max, row_sum, weighted = carried
        block_id, key_block, value_block = element
        scores = (
            jnp.einsum("qgae,kge->gaqk", queries, key_block, preferred_element_type=jnp.float32)
            * score_scale
        )
        key_pos = first_key + block_id * key_span + jnp.arange(key_span, dtype=jnp.int32)
        in_window = (
            (key_pos[None, :] <= query_pos[:, None])
            & (key_pos[None, :] > query_pos[:, None] - WINDOW)
            & (key_pos[None, :] >= 0)
        )
        new_max = jnp.maximum(row_max, jnp.max(jnp.where(in_window, scores, -jnp.inf), axis=-1))
        safe_max = jnp.where(new_max == -jnp.inf, 0.0, new_max)
        rescale = jnp.exp(row_max - safe_max)
        weight = jnp.where(in_window, jnp.exp(scores - safe_max[..., None]), 0.0)
        row_sum = row_sum * rescale + jnp.sum(weight, axis=-1)
        weighted = weighted * jnp.transpose(rescale, (2, 0, 1))[..., None] + jnp.einsum(
            "gaqk,kge->qgae",
            weight.astype(jnp.bfloat16),
            value_block,
            preferred_element_type=jnp.float32,
        )
        return ((new_max, row_sum, weighted), None)

    start_state = (
        jnp.full((kv_local, per_group, shard_len), -jnp.inf, jnp.float32),
        jnp.zeros((kv_local, per_group, shard_len), jnp.float32),
        jnp.zeros((shard_len, kv_local, per_group, head_dim), jnp.float32),
    )
    final_state = lax.scan(online_step, start_state, (block_ids, keys_all, values_all))[0]
    row_sum, weighted = (final_state[1], final_state[2])
    attended = (
        (weighted / jnp.transpose(row_sum, (2, 0, 1))[..., None])
        .reshape(shard_len, kv_local * per_group, head_dim)
        .astype(jnp.bfloat16)
    )
    target = lax.psum_scatter(
        jnp.einsum("the,hec->ct", attended, distill_proj, preferred_element_type=jnp.float32),
        ("role", "head"),
        scatter_dimension=0,
        tiled=True,
    )
    signal = conv_input.astype(jnp.float32)
    gate_part = gate_input.astype(jnp.float32)
    full_len = 2 * devices * shard_len
    seq_total = devices * shard_len
    freq_all = jnp.arange(2 * devices, dtype=jnp.int32)
    time_all = jnp.arange(shard_len, dtype=jnp.int32)
    part_len = shard_len // devices
    freq_mine = 2 * seq_rank + jnp.arange(2, dtype=jnp.int32)
    time_mine = seq_rank * part_len + jnp.arange(part_len, dtype=jnp.int32)

    def to_rows(stacked):
        return lax.all_to_all(stacked, "seq", split_axis=3, concat_axis=2, tiled=True)

    def to_cols(stacked):
        return lax.all_to_all(stacked, "seq", split_axis=2, concat_axis=3, tiled=True)

    def forward(stacked):
        pieces = stacked.shape[0]
        arrived = to_rows(stacked[:, :, None, :])
        real_part, imag_part = spread_rows(arrived)
        real_part, imag_part = twist(real_part, imag_part, freq_all, time_mine, full_len, -1.0)
        joined = to_cols(jnp.concatenate([real_part, imag_part], axis=0))
        return along_block(joined[:pieces], joined[pieces:], -1.0)

    def inverse(real_part, imag_part):
        pieces = real_part.shape[0]
        real_part, imag_part = along_block(real_part, imag_part, 1.0)
        real_part, imag_part = twist(real_part, imag_part, freq_mine, time_all, full_len, 1.0)
        arrived = to_rows(jnp.concatenate([real_part, imag_part], axis=0))
        rebuilt = gather_rows(arrived[:pieces], arrived[pieces:], full_len)
        return to_cols(rebuilt)[:, :, 0, :]

    grad_input, filter_step = student(
        signal, gate_part, filter_taps, target, skip_gain, forward, inverse, seq_total
    )
    return (grad_input, filter_step)


def half_step_table(length):
    product = np.arange(length)[:, None] * (2 * np.arange(length)[None, :] + 1) % (4 * length)
    angle = product * (math.pi / (2 * length))
    whole = np.concatenate([np.cos(angle), np.sin(angle)], axis=1)
    upper = whole.astype(ml_dtypes.bfloat16)
    lower = (whole - upper.astype(np.float64)).astype(ml_dtypes.bfloat16)
    return np.stack([upper, lower])


def fits_fused(query_heads, key_heads, value_heads, distill_proj, conv_input, gate_input, filter_taps, skip_gain):
    seq_total = lax.axis_size("seq") * query_heads.shape[0]
    groups = lax.axis_size("role") * lax.axis_size("head")
    chan_local = conv_input.shape[0]
    return (
        seq_total <= min(WINDOW, 1024)
        and query_heads.shape[0] % 128 == 0
        and key_heads.shape[1] == 1
        and key_heads.shape[2] % 128 == 0
        and chan_local % 128 == 0
        and chan_local * groups == distill_proj.shape[2]
    )


def dot_nt(left, right):
    return lax.dot_general(left, right, (((1,), (1,)), ((), ())), preferred_element_type=jnp.float32)


def forward(rows, table_buf, where):
    upper = jnp.dot(rows, table_buf[0, where, :], preferred_element_type=jnp.float32)
    return upper + jnp.dot(rows, table_buf[1, where, :], preferred_element_type=jnp.float32)


def inverse(spec, turned_buf):
    upper = spec.astype(jnp.bfloat16)
    lower = (spec - upper.astype(jnp.float32)).astype(jnp.bfloat16)
    width = turned_buf.shape[1] // 2
    wide = jnp.dot(upper, turned_buf[...], preferred_element_type=jnp.float32)
    rest = jnp.dot(lower, turned_buf[:, :width], preferred_element_type=jnp.float32)
    return wide[:, :width] + (wide[:, width:] + rest)


def fused_kernel(
    seq_n, role_n, head_n, heads,
    query_hbm, key_hbm, value_hbm, proj_hbm, signal_hbm, gate_hbm, taps_hbm, skip_hbm, table_hbm, turned_hbm,
    grad_ref, step_ref,
    query_buf, key_buf, value_buf, proj_buf, gate_buf, taps_buf, skip_buf, table_buf, turned_buf,
    pair_buf, spec_buf, out_buf, part_send, part_recv, back_buf,
    local_sem, gather_send, gather_recv, part_send_sem, part_recv_sem, back_send, back_recv,
):
    group_n = role_n * head_n
    mine = lax.axis_index("seq")
    group = lax.axis_index("role") * head_n + lax.axis_index("head")
    span = key_hbm.shape[0]
    chans = gate_buf.shape[0]
    seq_total = seq_n * span
    head_dim = key_hbm.shape[1]
    here = pl.ds(pl.multiple_of(mine * span, span), span)

    def place(rank):
        return pl.ds(pl.multiple_of(rank * span, span), span)

    def seq_peer(step):
        return lax.rem(mine + step, seq_n)

    def seq_from(step):
        return lax.rem(mine + seq_n - step, seq_n)

    def group_peer(step):
        other = lax.rem(group + step, group_n)
        return other, {"role": other // head_n, "head": lax.rem(other, head_n)}

    def group_from(step):
        return lax.rem(group + group_n - step, group_n)

    signal_rows, taps_rows = pl.ds(0, chans), pl.ds(chans, chans)
    locals_ = [
        pltpu.make_async_copy(source, target, local_sem.at[index])
        for index, (source, target) in enumerate([
            (taps_hbm, taps_buf),
            (query_hbm, query_buf),
            (key_hbm, key_buf.at[here]),
            (value_hbm, value_buf.at[here]),
            (signal_hbm, pair_buf.at[signal_rows, here]),
            (proj_hbm, proj_buf),
            (gate_hbm, gate_buf),
            (skip_hbm, skip_buf),
            (table_hbm, table_buf),
            (turned_hbm.at[:, pl.ds(pl.multiple_of(2 * mine * span, 2 * span), 2 * span)], turned_buf),
        ])
    ]
    for copy in locals_:
        copy.start()
    taps_copy, query_copy, key_copy, value_copy, signal_copy, proj_copy, gate_copy, skip_copy, table_copy, turned_copy = locals_

    barrier = pltpu.get_barrier_semaphore()
    for step in range(1, seq_n):
        pl.semaphore_signal(barrier, inc=1, device_id={"seq": seq_peer(step)}, device_id_type=MESH)
    for step in range(1, group_n):
        pl.semaphore_signal(barrier, inc=1, device_id=group_peer(step)[1], device_id_type=MESH)
    taps_copy.wait()
    pair_buf[taps_rows, here] = taps_buf[...].astype(jnp.bfloat16)
    rows = query_buf.shape[0]
    row_id = lax.broadcasted_iota(jnp.int32, (rows, rows), 0)
    col_id = lax.broadcasted_iota(jnp.int32, (rows, rows), 1)
    wanted = (row_id % span) * heads + row_id // span
    order = jnp.where(col_id == wanted, 1.0, 0.0).astype(jnp.bfloat16)
    query_copy.wait()
    queries = jnp.dot(order, query_buf[...], preferred_element_type=jnp.float32).astype(jnp.bfloat16)
    pl.semaphore_wait(barrier, seq_n + group_n - 2)

    gathered = (
        lambda owner: key_buf.at[place(owner)],
        lambda owner: value_buf.at[place(owner)],
        lambda owner: pair_buf.at[signal_rows, place(owner)],
        lambda owner: pair_buf.at[taps_rows, place(owner)],
    )
    sources = (key_hbm, value_hbm, signal_hbm, pair_buf.at[taps_rows, here])

    def gather(kind, index, owner, peer):
        return pltpu.make_async_remote_copy(
            src_ref=sources[kind],
            dst_ref=gathered[kind](owner),
            send_sem=gather_send.at[kind, index],
            recv_sem=gather_recv.at[kind, owner],
            device_id={"seq": peer},
            device_id_type=MESH,
        )

    far_first = sorted(range(1, seq_n), key=lambda step: abs(2 * step - seq_n))
    sends = []

    width = 2 if seq_n % 2 == 0 else 1

    def chunk(step):
        first = lax.rem(mine // width + step, seq_n // width) * width
        if step:
            owners = [first + inner for inner in range(width)]
        else:
            owners = [first + lax.rem(mine + 1, 2)] if width == 2 else []
        return first, owners, pl.ds(pl.multiple_of(first * span, width * span), width * span)

    def send_gather(kind, steps):
        for step in steps:
            for inner, peer in enumerate(chunk(step)[1]):
                copy = gather(kind, step * width + inner, mine, peer)
                copy.start()
                sends.append(copy)

    chunks = seq_n // width
    later = list(range(1, chunks))
    for kind in (0, 1):
        send_gather(kind, later + [0])
    for kind in (2, 3):
        send_gather(kind, [0])
    key_copy.wait()
    value_copy.wait()
    for step in range(seq_n // width):
        first, owners, where = chunk(step)
        for owner in owners:
            gather(0, 0, owner, owner).wait_recv()
        scores = dot_nt(queries, key_buf[where, :]) * (head_dim ** -0.5)
        query_pos = mine * span + lax.broadcasted_iota(jnp.int32, scores.shape, 0) % span
        key_pos = first * span + lax.broadcasted_iota(jnp.int32, scores.shape, 1)
        live = key_pos <= query_pos
        scores = jnp.where(live, scores, -jnp.inf)
        chunk_max = jnp.max(scores, axis=1, keepdims=True)
        new_max = jnp.maximum(row_max, chunk_max) if step else chunk_max
        weight = jnp.exp(scores - new_max)
        chunk_sum = jnp.sum(weight, axis=1, keepdims=True)
        for owner in owners:
            gather(1, 0, owner, owner).wait_recv()
        if step == chunks - 1:
            for kind in (2, 3):
                send_gather(kind, later)
        product = jnp.dot(weight.astype(jnp.bfloat16), value_buf[where, :], preferred_element_type=jnp.float32)
        if step:
            rescale = jnp.exp(row_max - new_max)
            row_sum = row_sum * rescale + chunk_sum
            weighted = weighted * rescale + product
        else:
            row_sum, weighted = chunk_sum, product
        row_max = new_max
        if step == 0:
            signal_copy.wait()
            table_copy.wait()
            for owner in owners:
                gather(2, 0, owner, owner).wait_recv()
                gather(3, 0, owner, owner).wait_recv()
            spec_buf[...] = forward(pair_buf[:, where], table_buf, where)
    attended = (weighted / row_sum).astype(jnp.bfloat16)

    attended = jnp.concatenate([attended[head * span:(head + 1) * span] for head in range(heads)], axis=1)
    proj_copy.wait()
    def part_copy(other, slot):
        return pltpu.make_async_remote_copy(
            src_ref=part_send.at[other],
            dst_ref=part_recv.at[slot],
            send_sem=part_send_sem.at[other],
            recv_sem=part_recv_sem.at[slot],
            device_id={"role": other // head_n, "head": lax.rem(other, head_n)},
            device_id_type=MESH,
        )

    couple = 2 if group_n % 2 == 0 else 1
    for step in list(range(1, group_n // couple, 2)) + list(range(2, group_n // couple, 2)) + [0]:
        first = lax.rem(group // couple + step, group_n // couple) * couple
        columns = pl.ds(pl.multiple_of(first * chans, couple * chans), couple * chans)
        partial = jnp.dot(attended, proj_buf[:, columns], preferred_element_type=jnp.float32)
        for inner in range(couple):
            part_send[first + inner] = partial[:, inner * chans:(inner + 1) * chans].astype(jnp.bfloat16)
        if step:
            others = [first + inner for inner in range(couple)]
        else:
            others = [first + lax.rem(group + 1, 2)] if couple == 2 else []
        for other in others:
            copy = part_copy(other, group)
            copy.start()
            sends.append(copy)

    turned_copy.wait()
    gate_copy.wait()
    skip_copy.wait()
    for step in later:
        _, owners, where = chunk(step)
        for owner in owners:
            gather(2, 0, owner, owner).wait_recv()
            gather(3, 0, owner, owner).wait_recv()
        spec_buf[...] += forward(pair_buf[:, where], table_buf, where)
    low, high = pl.ds(0, seq_total), pl.ds(seq_total, seq_total)
    input_c, input_s = spec_buf[signal_rows, low], spec_buf[signal_rows, high]
    taps_c, taps_s = spec_buf[taps_rows, low], spec_buf[taps_rows, high]
    conv_spec = jnp.concatenate(
        [input_c * taps_c - input_s * taps_s, input_c * taps_s + input_s * taps_c], axis=1
    )
    conv = inverse(conv_spec, turned_buf) * (1.0 / seq_total)
    skip = jnp.transpose(jnp.broadcast_to(skip_buf[...], (span, chans)))
    gate = gate_buf[...].astype(jnp.float32)
    out_buf[...] = gate * (conv + skip * pair_buf[signal_rows, here].astype(jnp.float32))

    target = part_send[group].astype(jnp.float32)
    for step in range(1, group_n):
        source = group_from(step)
        part_copy(source, source).wait_recv()
        target = target + part_recv[source].astype(jnp.float32)
    back = gate * (out_buf[...] - jnp.transpose(target))
    back_buf[:, here] = back.astype(jnp.bfloat16)

    def back_copy(step, owner):
        where = place(owner)
        return pltpu.make_async_remote_copy(
            src_ref=back_buf.at[:, here],
            dst_ref=back_buf.at[:, where],
            send_sem=back_send.at[step],
            recv_sem=back_recv.at[owner],
            device_id={"seq": seq_peer(step)},
            device_id_type=MESH,
        )

    for step in far_first:
        copy = back_copy(step, mine)
        copy.start()
        sends.append(copy)
    back_spec = 0.0
    for step in range(seq_n // width):
        _, owners, where = chunk(step)
        for owner in owners:
            back_copy(1, owner).wait_recv()
        back_spec = back_spec + forward(back_buf[:, where], table_buf, where)
    back_c, back_s = back_spec[:, :seq_total], back_spec[:, seq_total:]

    def correlation(rows):
        first_c, first_s = spec_buf[rows, low], spec_buf[rows, high]
        return jnp.concatenate([first_c * back_c + first_s * back_s, first_c * back_s - first_s * back_c], axis=1)

    lags = inverse(jnp.concatenate([correlation(taps_rows), correlation(signal_rows)], axis=0), turned_buf)
    grad_ref[...] = skip * back + lags[:chans] * (1.0 / seq_total)
    step_ref[...] = lags[chans:] * (seq_total ** -1.5)
    for copy in sends:
        copy.wait_send()


def hand_over(grad_in, step_in, grad_out, step_out, sems):
    copies = [
        pltpu.make_async_copy(grad_in, grad_out, sems.at[0]),
        pltpu.make_async_copy(step_in, step_out, sems.at[1]),
    ]
    for copy in copies:
        copy.start()
    for copy in copies:
        copy.wait()


def fused_body(query_heads, key_heads, value_heads, distill_proj, conv_input, gate_input, filter_taps, skip_gain):
    span, heads, head_dim = query_heads.shape
    seq_n, role_n, head_n = (lax.axis_size(axis) for axis in ("seq", "role", "head"))
    group_n = role_n * head_n
    seq_total = seq_n * span
    chans = conv_input.shape[0]
    table_terms = half_step_table(seq_total)
    table = jnp.asarray(table_terms)
    turned = table_terms.reshape(2, seq_n, span, 2 * seq_total).transpose(3, 1, 0, 2)
    turned = jnp.asarray(np.ascontiguousarray(turned.reshape(2 * seq_total, 2 * seq_total)))
    in_hbm = pl.BlockSpec(memory_space=pltpu.HBM)
    vmem = pl.BlockSpec(memory_space=pltpu.VMEM)
    bf16, f32 = jnp.bfloat16, jnp.float32
    dma = pltpu.SemaphoreType.DMA
    operands = (
        query_heads.reshape(span * heads, head_dim),
        key_heads.reshape(span, head_dim),
        value_heads.reshape(span, head_dim),
        distill_proj.reshape(heads * head_dim, distill_proj.shape[2]),
        conv_input,
        gate_input,
        filter_taps,
        skip_gain.reshape(1, chans),
        table,
        turned,
    )
    results = pl.pallas_call(
        functools.partial(fused_kernel, seq_n, role_n, head_n, heads),
        out_shape=[pltpu.VMEM((chans, span), f32)] * 2,
        in_specs=[in_hbm] * 10,
        out_specs=[vmem, vmem],
        scratch_shapes=[
            pltpu.VMEM((span * heads, head_dim), bf16),
            pltpu.VMEM((seq_total, head_dim), bf16),
            pltpu.VMEM((seq_total, head_dim), bf16),
            pltpu.VMEM((heads * head_dim, distill_proj.shape[2]), bf16),
            pltpu.VMEM((chans, span), bf16),
            pltpu.VMEM((chans, span), f32),
            pltpu.VMEM((1, chans), f32),
            pltpu.VMEM(table.shape, bf16),
            pltpu.VMEM((2 * seq_total, 2 * span), bf16),
            pltpu.VMEM((2 * chans, seq_total), bf16),
            pltpu.VMEM((2 * chans, 2 * seq_total), f32),
            pltpu.VMEM((chans, span), f32),
            pltpu.VMEM((group_n, span, chans), bf16),
            pltpu.VMEM((group_n, span, chans), bf16),
            pltpu.VMEM((chans, seq_total), bf16),
            dma((10,)),
            dma((4, seq_n)),
            dma((4, seq_n)),
            dma((group_n,)),
            dma((group_n,)),
            dma((seq_n,)),
            dma((seq_n,)),
        ],
        compiler_params=pltpu.CompilerParams(
            collective_id=0, has_side_effects=True, vmem_limit_bytes=40 * 1024 * 1024
        ),
    )(*[pltpu.with_memory_space_constraint(operand, pltpu.HBM) for operand in operands])
    return pl.pallas_call(
        hand_over,
        out_shape=[jax.ShapeDtypeStruct((chans, span), f32)] * 2,
        in_specs=[pl.BlockSpec(memory_space=pl.ANY)] * 2,
        out_specs=[in_hbm] * 2,
        scratch_shapes=[dma((2,))],
        compiler_params=pltpu.CompilerParams(vmem_limit_bytes=40 * 1024 * 1024),
    )(*results)


def solution(mesh):
    in_specs = (
        P("seq", ("role", "head"), None),
        P("seq", ("role", "head"), None),
        P("seq", ("role", "head"), None),
        P(("role", "head"), None, None),
        P(("role", "head"), "seq"),
        P(("role", "head"), "seq"),
        P(("role", "head"), "seq"),
        P(("role", "head")),
    )
    out_specs = (P(("role", "head"), "seq"), P(("role", "head"), "seq"))
    def chosen(*arrays):
        return fused_body(*arrays) if fits_fused(*arrays) else body(*arrays)

    return jax.shard_map(chosen, mesh=mesh, in_specs=in_specs, out_specs=out_specs, check_vma=False)
```
